32 devices in a mesh: trainer: 8 (over y, x, core), depth: 4 (over z).
Axes of the slice: x: 2, y: 2, z: 4, core: 2. Of those that a mesh axis runs over, the one named last changes fastest.
Arguments:
- noise: bfloat16 [8, 16, 64, 256], P('trainer', 'depth'), may hold values from -6 to 6
- gen_weight: float32 [8, 331776], P('trainer', 'depth'), may hold values from -0.15625 to 0.15625
- gen_momentum: float32 [8, 331776], P('trainer', 'depth'), may hold values from -6 to 6
- disc_weight: bfloat16 [8, 8, 128, 64], P('trainer'), may hold values from -0.25 to 0.25
- score_weight: float32 [8, 128], P('trainer'), may hold values from -0.5 to 0.5
- pairing: int32 [8], replicated, may hold values from 0 to 7, as said below
- flags: int32 [8], replicated, may hold values from 0 to 1, as said below
Outputs:
- generated: bfloat16 [8, 16, 64, 256], P('trainer', 'depth')
- new_weight: float32 [8, 331776], P('trainer', 'depth')
- new_momentum: float32 [8, 331776], P('trainer', 'depth')
The draws below stay inside these ranges and needn't reach their ends.
Inputs may be any that keep to these rules, and one draw needn't show every extreme that they name: pairing is a perfect matching: pairing[pairing[i]] == i and pairing[i] != i for every trainer. `flags`: in every matched pair exactly one trainer has flag 1.
All inputs are finite; a program needn't handle non-finite values.
Results may differ from the reference program's by a relative error of at most 0.013.
Values may be sent and summed in bfloat16 or wider, within the bound.
A program may use at most 64 MiB of HBM per device.

```python
import jax
import jax.numpy as jnp
import numpy as np
from jax import lax

C = 64
DC = 128
Y = 2
X = 128
YX = 256
TRAINERS = 8
NZ = 16
GEN_PARAMS = 331776


def pairing_helper(key):
    folded = jax.random.fold_in(key, 11)
    half = TRAINERS // 2
    rotation = jax.random.randint(jax.random.fold_in(folded, 1), (), 0, TRAINERS).astype(jnp.int32)
    rest_offsets = jnp.asarray(np.array([k for k in range(3, TRAINERS) if k != half], dtype=np.int32))
    shuffled = jax.random.permutation(jax.random.fold_in(folded, 2), rest_offsets)
    fixed_offsets = jnp.array([0, half, 1, 2], dtype=jnp.int32)
    order = (rotation + jnp.concatenate([fixed_offsets, shuffled.astype(jnp.int32)])) % TRAINERS
    order = order.astype(jnp.int32)
    firsts = order[0::2]
    seconds = order[1::2]
    partner_ids = jnp.zeros((TRAINERS,), jnp.int32).at[firsts].set(seconds).at[seconds].set(firsts)
    coin_flips = jax.random.randint(jax.random.fold_in(folded, 3), (half,), 0, 2).astype(jnp.int32)
    coin_flips = coin_flips.at[1].set(1)
    winner_flags = jnp.zeros((TRAINERS,), jnp.int32).at[firsts].set(coin_flips).at[seconds].set(1 - coin_flips)
    return (partner_ids.astype(jnp.int32), winner_flags.astype(jnp.int32))


def draw_pairing(key, part):
    return pairing_helper(key)[0]


def draw_flags(key, part):
    return pairing_helper(key)[1]


def block_scale(key, extent, cuts, smallest, largest):
    gain = 1.0
    for dim, shards_of in cuts:
        steps = jax.random.uniform(jax.random.fold_in(jax.random.fold_in(key, 6), dim), (shards_of,), jnp.float32, smallest / len(cuts), largest / len(cuts))
        gain = gain * jnp.repeat(jnp.exp(steps), extent[dim] // shards_of).reshape((-1,) + (1,) * (len(extent) - 1 - dim))
    return gain


def bell_draw(stream_key, extent, width, most, pieces=(), kind=jnp.bfloat16):
    entries = width * jax.random.normal(stream_key, extent, jnp.float32)
    if pieces:
        entries = entries * block_scale(stream_key, extent, pieces, -0.22, 0.18)
    return jnp.clip(entries, -most, most).astype(kind)


def setup_inputs(seed: int = 0) -> dict:
    keys = jax.random.split(jax.random.key(seed), 8)
    return {
        "noise": bell_draw(keys[0], (TRAINERS, NZ, C, YX), 1.0, 6.0, ((0, 8), (1, 4))),
        "gen_weight": bell_draw(keys[1], (TRAINERS, GEN_PARAMS), (27 * C) ** -0.5, 0.15625, ((0, 8), (1, 4)), jnp.float32),
        "gen_momentum": bell_draw(keys[2], (TRAINERS, GEN_PARAMS), 1.0, 6.0, ((0, 8), (1, 4)), jnp.float32),
        "disc_weight": bell_draw(keys[3], (TRAINERS, 8, DC, C), (8 * C) ** -0.5, 0.25, ((0, 8),)),
        "score_weight": bell_draw(keys[4], (TRAINERS, DC), DC ** -0.5, 0.5, ((0, 8),), jnp.float32),
        "pairing": draw_pairing(jax.random.fold_in(keys[7], 71), 0),
        "flags": draw_flags(jax.random.fold_in(keys[7], 71), 0),
    }


shift_table = [(shift_z, shift_y, shift_x) for shift_z in range(3) for shift_y in range(3) for shift_x in range(3)]
momentum_decay = 0.9
step_length = 0.01

def frame_all(volume):
    return jnp.pad(volume, ((0, 0), (1, 1), (1, 1), (1, 1)))

def convolve(volume, kernel):
    framed = frame_all(volume).astype(jnp.float32)
    planes, height, breadth = (volume.shape[1], volume.shape[2], volume.shape[3])
    summed = jnp.zeros((kernel.shape[1], planes, height, breadth), jnp.float32)
    for position, (shift_z, shift_y, shift_x) in enumerate(shift_table):
        window = framed[:, shift_z:shift_z + planes, shift_y:shift_y + height, shift_x:shift_x + breadth]
        summed = summed + jnp.einsum('oi,izyx->ozyx', kernel[position].astype(jnp.float32), window)
    return summed

def convolve_back(gradient, kernel):
    framed = frame_all(gradient).astype(jnp.float32)
    planes, height, breadth = (gradient.shape[1], gradient.shape[2], gradient.shape[3])
    summed = jnp.zeros((kernel.shape[2], planes, height, breadth), jnp.float32)
    for position, (shift_z, shift_y, shift_x) in enumerate(shift_table):
        window = framed[:, 2 - shift_z:2 - shift_z + planes, 2 - shift_y:2 - shift_y + height, 2 - shift_x:2 - shift_x + breadth]
        summed = summed + jnp.einsum('oi,ozyx->izyx', kernel[position].astype(jnp.float32), window)
    return summed

def kernel_grad(gradient, volume):
    framed = frame_all(volume).astype(jnp.float32)
    planes, height, breadth = (volume.shape[1], volume.shape[2], volume.shape[3])
    upstream = gradient.astype(jnp.float32)
    pieces_list = []
    for shift_z, shift_y, shift_x in shift_table:
        window = framed[:, shift_z:shift_z + planes, shift_y:shift_y + height, shift_x:shift_x + breadth]
        pieces_list.append(jnp.einsum('ozyx,izyx->oi', upstream, window))
    return jnp.stack(pieces_list)

def gelu_back(inputs, upstream):
    return jax.vjp(jax.nn.gelu, inputs)[1](upstream)[0]

def critic_grad(generated, disc_kernel, score_vector):
    channels, planes, height, breadth = generated.shape
    blocks = generated.reshape(channels, planes // 2, 2, height // 2, 2, breadth // 2, 2).astype(jnp.float32)
    kernel_cube = disc_kernel.reshape(2, 2, 2, disc_kernel.shape[1], channels).astype(jnp.float32)
    response = jnp.einsum('abdoc,czaybxd->ozyx', kernel_cube, blocks)
    features = jax.nn.gelu(response)
    scores = lax.optimization_barrier(jnp.sum(score_vector[:, None, None, None] * features, axis=0))
    slope = -jax.nn.sigmoid(-scores)
    upstream = gelu_back(response, slope[None] * score_vector[:, None, None, None]).astype(jnp.bfloat16)
    spread = jnp.einsum('abdoc,ozyx->czaybxd', kernel_cube, upstream.astype(jnp.float32))
    return spread.reshape(channels, planes, height, breadth)

def one_trainer(inputs):
    stored, weight_row, disc_kernel, score_vector = inputs
    planes_all, channels = (stored.shape[0], stored.shape[1])
    latent = stored.reshape(planes_all, channels, Y, X).transpose(1, 0, 2, 3)
    layers = weight_row.astype(jnp.bfloat16).reshape(3, 27, channels, channels)
    first_pre = convolve(latent, layers[0])
    first_act = jax.nn.gelu(first_pre).astype(jnp.bfloat16)
    second_pre = convolve(first_act, layers[1])
    second_act = jax.nn.gelu(second_pre).astype(jnp.bfloat16)
    third_pre = convolve(second_act, layers[2])
    output_f = jnp.tanh(third_pre)
    generated = output_f.astype(jnp.bfloat16)
    gen_grad = critic_grad(generated, disc_kernel, score_vector)
    third_grad = (gen_grad * (1.0 - output_f * output_f)).astype(jnp.bfloat16)
    grad_three = kernel_grad(third_grad, second_act)
    second_back = convolve_back(third_grad, layers[2])
    second_grad = gelu_back(second_pre, second_back).astype(jnp.bfloat16)
    grad_two = kernel_grad(second_grad, first_act)
    first_back = convolve_back(second_grad, layers[1])
    first_grad = gelu_back(first_pre, first_back).astype(jnp.bfloat16)
    grad_one = kernel_grad(first_grad, latent)
    weight_grad = jnp.concatenate([grad_one.reshape(-1), grad_two.reshape(-1), grad_three.reshape(-1)])
    generated_out = generated.transpose(1, 0, 2, 3).reshape(planes_all, channels, Y * X)
    return (generated_out, weight_grad)

def reference(noise, gen_weight, gen_momentum, disc_weight, score_weight, pairing, flags):
    keeper = (flags == 1)[:, None]
    chosen_weight = jnp.where(keeper, gen_weight, gen_weight[pairing])
    chosen_momentum = jnp.where(keeper, gen_momentum, gen_momentum[pairing])
    generated, weight_grad = lax.map(one_trainer, (noise, chosen_weight, disc_weight, score_weight))
    new_momentum = momentum_decay * chosen_momentum + weight_grad
    new_weight = chosen_weight - step_length * new_momentum
    return (generated, new_weight, new_momentum)
```

```python
import functools

import jax
import jax.numpy as jnp
from jax import lax
from jax.experimental import pallas as pl
from jax.experimental.pallas import tpu as pltpu
from jax.sharding import PartitionSpec as P

Y = 2
X = 128


momentum_decay = 0.9
step_length = 0.01


def extended(block, sides, width):
    for axis, dim in sides:
        count = lax.axis_size(axis)
        forward = [(i, i + 1) for i in range(count - 1)]
        backward = [(target, source) for source, target in forward]
        low = lax.ppermute(
            lax.slice_in_dim(block, block.shape[dim] - width, None, axis=dim), axis, forward
        )
        high = lax.ppermute(lax.slice_in_dim(block, 0, width, axis=dim), axis, backward)
        block = jnp.concatenate([low, block, high], axis=dim)
    return block


def framed_copies(padded):
    breadth = X
    cells = padded.shape[2]
    framed = jnp.pad(padded, ((0, 0), (0, 0), (breadth + 1, breadth + 1)))
    column = (jnp.arange(cells + 2 * breadth + 2, dtype=jnp.int32) - breadth - 1) % breadth
    left_copy = jnp.where(
        (column == breadth - 1)[None, None, :], jnp.zeros((), framed.dtype), framed
    )
    right_copy = jnp.where((column == 0)[None, None, :], jnp.zeros((), framed.dtype), framed)
    return (left_copy, framed, right_copy)


def stacked_window(copies, read_y, cells):
    breadth = X
    parts_list = []
    for read_x in range(3):
        begin = read_y * breadth + read_x
        parts_list.append(copies[read_x][:, :, begin : begin + cells])
    return jnp.concatenate(parts_list, axis=1)


def group_kernel(layer):
    channels = layer.shape[-1]
    cube = layer.reshape(3, 3, 3, channels, channels)
    return cube.transpose(0, 1, 3, 2, 4).reshape(3, 3, channels, 3 * channels)


def flip_kernel(layer):
    channels = layer.shape[-1]
    cube = layer.reshape(3, 3, 3, channels, channels)[::-1, ::-1, ::-1].swapaxes(3, 4)
    return cube.transpose(0, 1, 3, 2, 4).reshape(3, 3, channels, 3 * channels)


def convolve_grouped(padded, grouped):
    planes, cells = (padded.shape[0] - 2, padded.shape[2])
    copies = framed_copies(padded)
    summed = jnp.zeros((planes, grouped.shape[2], cells), jnp.float32)
    for read_y in range(3):
        window = stacked_window(copies, read_y, cells)
        for read_z in range(3):
            summed = summed + jnp.einsum(
                "oj,zjs->zos",
                grouped[read_z, read_y],
                window[read_z : read_z + planes],
                preferred_element_type=jnp.float32,
            )
    return summed


def convolve(padded, layer):
    return convolve_grouped(padded, group_kernel(layer))


def convolve_back(padded, layer):
    return convolve_grouped(padded, flip_kernel(layer))


def kernel_grad(gradient, padded):
    planes, channels_out, cells = gradient.shape
    channels_in = padded.shape[1]
    copies = framed_copies(padded)
    rows_list = []
    for read_z in range(3):
        row_list = []
        for read_y in range(3):
            window = stacked_window(copies, read_y, cells)
            row_list.append(
                jnp.einsum(
                    "zos,zjs->oj",
                    gradient,
                    window[read_z : read_z + planes],
                    preferred_element_type=jnp.float32,
                )
            )
        rows_list.append(jnp.stack(row_list))
    grouped = jnp.stack(rows_list)
    return (
        grouped.reshape(3, 3, channels_out, 3, channels_in)
        .transpose(0, 1, 3, 2, 4)
        .reshape(27, channels_out, channels_in)
    )


def gelu_back(inputs, upstream):
    return jax.vjp(jax.nn.gelu, inputs)[1](upstream)[0]


def widen_back(gradient):
    return extended(gradient, (("depth", 0),), 1)


def widen_forward(volume):
    return extended(volume, (("depth", 0),), 1)


def critic_grad(generated, disc_kernel, score_vector):
    planes, channels, cells = generated.shape
    blocks = generated.reshape(planes // 2, 2, channels, Y // 2, 2, X // 2, 2)
    kernel_cube = disc_kernel.reshape(2, 2, 2, disc_kernel.shape[1], channels)
    response = jnp.einsum(
        "abdoc,zacybxd->zoyx", kernel_cube, blocks, preferred_element_type=jnp.float32
    )
    features = jax.nn.gelu(response)
    scores = jnp.sum(score_vector[None, :, None, None] * features, axis=1)
    slope = -jax.nn.sigmoid(-scores)
    upstream = gelu_back(response, slope[:, None] * score_vector[None, :, None, None]).astype(
        jnp.bfloat16
    )
    spread = jnp.einsum(
        "abdoc,zoyx->zacybxd", kernel_cube, upstream, preferred_element_type=jnp.float32
    )
    return spread.reshape(planes, channels, cells)


def on_device_split(noise, gen_weight, gen_momentum, disc_weight, score_weight, pairing, flags):
    trainer_rank = lax.axis_index("trainer")
    partner = pairing[trainer_rank]
    keeper = flags[trainer_rank] == 1
    trainer_count = lax.axis_size("trainer")
    own_pair = jnp.concatenate([gen_weight, gen_momentum], axis=0)
    slot_ids = jnp.arange(trainer_count, dtype=jnp.int32)
    outgoing = jnp.where((slot_ids == partner)[:, None, None], own_pair[None], 0.0)
    incoming = lax.all_to_all(
        outgoing.astype(jnp.bfloat16), "trainer", split_axis=0, concat_axis=0, tiled=True
    ).astype(outgoing.dtype)
    arrived = lax.dynamic_index_in_dim(incoming, partner, 0, keepdims=False)
    other_weight, other_moment = (arrived[0:1], arrived[1:2])
    chosen_weight = jnp.where(keeper, gen_weight, other_weight)
    chosen_momentum = jnp.where(keeper, gen_momentum, other_moment)
    channels = noise.shape[2]
    all_kernels = lax.all_gather(chosen_weight.astype(jnp.bfloat16), "depth", axis=1, tiled=True)
    layers = all_kernels.reshape(3, 27, channels, channels)
    latent = noise[0]
    latent_pad = widen_forward(latent)
    first_pre = convolve(latent_pad, layers[0])
    first_act_pad = widen_forward(jax.nn.gelu(first_pre).astype(jnp.bfloat16))
    second_pre = convolve(first_act_pad, layers[1])
    second_act_pad = widen_forward(jax.nn.gelu(second_pre).astype(jnp.bfloat16))
    third_pre = convolve(second_act_pad, layers[2])
    output_f = jnp.tanh(third_pre)
    generated = output_f.astype(jnp.bfloat16)
    gen_grad = critic_grad(generated, disc_weight[0], score_weight[0])
    third_grad = (gen_grad * (1.0 - output_f * output_f)).astype(jnp.bfloat16)
    grad_three = kernel_grad(third_grad, second_act_pad)
    second_back = convolve_back(widen_back(third_grad), layers[2])
    second_grad = gelu_back(second_pre, second_back).astype(jnp.bfloat16)
    grad_two = kernel_grad(second_grad, first_act_pad)
    first_back = convolve_back(widen_back(second_grad), layers[1])
    first_grad = gelu_back(first_pre, first_back).astype(jnp.bfloat16)
    grad_one = kernel_grad(first_grad, latent_pad)
    local_grad = jnp.concatenate(
        [grad_one.reshape(-1), grad_two.reshape(-1), grad_three.reshape(-1)]
    )
    share_len = gen_weight.shape[1]
    grad_whole = lax.psum(local_grad.astype(jnp.bfloat16), "depth").astype(jnp.float32)
    grad_share = lax.dynamic_slice_in_dim(
        grad_whole, lax.axis_index("depth") * share_len, share_len, 0
    )
    new_momentum = momentum_decay * chosen_momentum + grad_share[None, :]
    new_weight = chosen_weight - step_length * new_momentum
    return (generated[None], new_weight, new_momentum)


MESH = pl.DeviceIdType.MESH
VMEM_LIMIT = 56 * 1024 * 1024
WHOLE_PLANES = 16


def bit_orders(count):
    bits = [1 << k for k in range(count.bit_length() - 1)]
    return bits[1:] + bits[:1], bits[:0:-1] + bits[:1]


def flipped(index, bit):
    return index + bit - 2 * bit * lax.rem(index // bit, 2)


def doubling(slots, order, rank, send_sem, recv_sem):
    for k, bit in enumerate(order):
        copy = pltpu.make_async_remote_copy(
            src_ref=slots.at[pl.ds(0, 1 << k)],
            dst_ref=slots.at[pl.ds(1 << k, 1 << k)],
            send_sem=send_sem.at[k],
            recv_sem=recv_sem.at[k],
            device_id={"trainer": flipped(rank, bit)},
            device_id_type=MESH,
        )
        copy.start()
        yield
        copy.wait()


def line_gather(slots, place, count, up_send, up_recv, down_send, down_recv):
    def move(slot, target, send_sem, recv_sem):
        return pltpu.make_async_remote_copy(
            src_ref=slots.at[slot],
            dst_ref=slots.at[slot],
            send_sem=send_sem,
            recv_sem=recv_sem,
            device_id={"depth": target},
            device_id_type=MESH,
        )

    def up(step):
        return move(jnp.maximum(place - step, 0), place + 1, up_send.at[step], up_recv.at[step])

    def down(step):
        return move(
            jnp.minimum(place + step, count - 1), place - 1, down_send.at[step], down_recv.at[step]
        )

    for step in range(count - 1):

        @pl.when((place < count - 1) & (place >= step))
        def _():
            up(step).start()

        @pl.when((place > 0) & (place + step <= count - 1))
        def _():
            down(step).start()

        yield

        @pl.when(place >= step + 1)
        def _():
            up(step).wait_recv()

        @pl.when(place + step + 1 <= count - 1)
        def _():
            down(step).wait_recv()

    for step in range(count - 1):

        @pl.when((place < count - 1) & (place >= step))
        def _():
            up(step).wait_send()

        @pl.when((place > 0) & (place + step <= count - 1))
        def _():
            down(step).wait_send()


def advance(*steps):
    alive = False
    for each in steps:
        alive = next(each, 0) is None or alive
    return alive


def exchange_kernel(
    trainers,
    depth,
    pick_ref,
    weight_ref,
    moment_ref,
    noise_ref,
    kernels_ref,
    volume_ref,
    near_weight_ref,
    near_moment_ref,
    weight_a,
    weight_b,
    moment_a,
    moment_b,
    send_sem,
    recv_sem,
    line_sem,
):
    rank = lax.axis_index("trainer")
    place = lax.axis_index("depth")
    order_a, order_b = bit_orders(trainers)
    barrier = pltpu.get_barrier_semaphore()
    for bit in order_a:
        pl.semaphore_signal(
            barrier, inc=1, device_id={"trainer": flipped(rank, bit)}, device_id_type=MESH
        )

    @pl.when(place > 0)
    def _():
        pl.semaphore_signal(barrier, inc=1, device_id={"depth": place - 1}, device_id_type=MESH)

    @pl.when(place < depth - 1)
    def _():
        pl.semaphore_signal(barrier, inc=1, device_id={"depth": place + 1}, device_id_type=MESH)

    half = weight_a.shape[1]
    padding = jnp.zeros((2 * half - weight_ref.shape[0], weight_ref.shape[1]), jnp.float32)
    weight_a[0] = weight_ref[:half].astype(jnp.bfloat16)
    weight_b[0] = jnp.concatenate([weight_ref[half:], padding], axis=0).astype(jnp.bfloat16)
    moment_a[0] = moment_ref[:half].astype(jnp.bfloat16)
    moment_b[0] = jnp.concatenate([moment_ref[half:], padding], axis=0).astype(jnp.bfloat16)
    volume_ref[place] = noise_ref[...]

    beside = (place > 0).astype(jnp.int32) + (place < depth - 1).astype(jnp.int32)
    pl.semaphore_wait(barrier, len(order_a) + beside)

    planes = line_gather(
        volume_ref, place, depth, line_sem.at[0], line_sem.at[1], line_sem.at[2], line_sem.at[3]
    )
    first = doubling(weight_a, order_a, rank, send_sem.at[0], recv_sem.at[0])
    second = doubling(weight_b, order_b, rank, send_sem.at[1], recv_sem.at[1])
    advance(first, second, planes)
    while advance(first, second):
        advance(planes)

    near_weight_ref[:half] = weight_a[pick_ref[0]]
    near_weight_ref[half:] = weight_b[pick_ref[1]]
    kernels_ref[place] = near_weight_ref[...]
    share = line_gather(
        kernels_ref, place, depth, line_sem.at[4], line_sem.at[5], line_sem.at[6], line_sem.at[7]
    )
    third = doubling(moment_a, order_a, rank, send_sem.at[2], recv_sem.at[2])
    fourth = doubling(moment_b, order_b, rank, send_sem.at[3], recv_sem.at[3])
    advance(share, third, fourth)
    while advance(planes):
        pass
    while advance(share, third, fourth):
        pass
    near_moment_ref[:half] = moment_a[pick_ref[0]]
    near_moment_ref[half:] = moment_b[pick_ref[1]]


def exchange(trainers, depth, picks, weight, moment, noise):
    rows = weight.shape[0]
    half = -(-rows // 32) * 16
    levels = trainers.bit_length() - 1
    vmem = pl.BlockSpec(memory_space=pltpu.VMEM)
    slots = pltpu.VMEM((trainers, half, X), jnp.bfloat16)
    near = jax.ShapeDtypeStruct((2 * half, X), jnp.bfloat16)
    return pl.pallas_call(
        functools.partial(exchange_kernel, trainers, depth),
        out_shape=(
            jax.ShapeDtypeStruct((depth, 2 * half, X), jnp.bfloat16),
            jax.ShapeDtypeStruct((depth,) + noise.shape, jnp.bfloat16),
            near,
            near,
        ),
        in_specs=[pl.BlockSpec(memory_space=pltpu.SMEM), vmem, vmem, vmem],
        out_specs=(vmem,) * 4,
        scratch_shapes=[
            slots,
            slots,
            slots,
            slots,
            pltpu.SemaphoreType.DMA((4, levels)),
            pltpu.SemaphoreType.DMA((4, levels)),
            pltpu.SemaphoreType.DMA((8, depth - 1)),
        ],
        compiler_params=pltpu.CompilerParams(
            collective_id=0, has_side_effects=True, vmem_limit_bytes=VMEM_LIMIT
        ),
    )(picks, weight, moment, noise)


ROOT = 0.7978845608028654
CUBIC = 0.044715


def gelu_of(inputs):
    bend = jnp.tanh(ROOT * (inputs + CUBIC * (inputs * inputs * inputs)))
    return 0.5 * inputs * (1.0 + bend)


def gelu_slope(inputs):
    square = inputs * inputs
    bend = jnp.tanh(ROOT * (inputs + CUBIC * (square * inputs)))
    tilt = ROOT * (1.0 + 3.0 * CUBIC * square)
    return 0.5 * (1.0 + bend) + 0.5 * inputs * (1.0 - bend * bend) * tilt


def dot(left, right):
    return jnp.dot(left, right, preferred_element_type=jnp.float32)


def dot_rows(left, right):
    return lax.dot_general(
        left, right, (((1,), (1,)), ((), ())), preferred_element_type=jnp.float32
    )


def trainer_kernel(
    planes,
    pick_ref,
    kernels_ref,
    noise_ref,
    disc_ref,
    score_ref,
    weight_ref,
    moment_ref,
    near_weight_ref,
    near_moment_ref,
    made_ref,
    new_weight_ref,
    new_moment_ref,
    square_ref,
    fore_ref,
    back_ref,
    inputs_ref,
    grads_ref,
    pre_ref,
    made_all,
):
    channels = noise_ref.shape[1]
    wide = 2 * channels
    cells = planes * X
    shares, share_rows = kernels_ref.shape[0], weight_ref.shape[0]
    lane = lax.broadcasted_iota(jnp.int32, (wide, X), 1)

    def put(buffer, plane, value):
        columns = pl.ds(pl.multiple_of((plane + 1) * X, X), X)
        low = jnp.where(lane == 0, 0.0, pltpu.roll(value, 1, 1))
        high = jnp.where(lane == X - 1, 0.0, pltpu.roll(value, X - 1, 1))
        buffer[0:wide, columns] = low.astype(jnp.bfloat16)
        buffer[wide : 2 * wide, columns] = value.astype(jnp.bfloat16)
        buffer[2 * wide : 3 * wide, columns] = high.astype(jnp.bfloat16)

    empty = jnp.zeros((3 * wide, X), jnp.bfloat16)
    for buffer in [inputs_ref.at[k] for k in range(3)] + [grads_ref.at[k] for k in range(2)]:
        buffer[:, 0:X] = empty
        buffer[:, cells + X : cells + 2 * X] = empty

    for part in range(shares):
        rows = kernels_ref[part].astype(jnp.float32)[:share_rows]
        begin = 2 * part * share_rows
        square_ref[pl.ds(begin, share_rows, stride=2), :] = rows[:, :channels]
        square_ref[pl.ds(begin + 1, share_rows, stride=2), :] = rows[:, channels:]

    def tap(layer, a, b, c):
        begin = (27 * layer + 9 * a + 3 * b + c) * channels
        return square_ref[begin : begin + channels, :]

    for layer in range(3):
        for a in range(3):
            for c in range(3):
                middle = tap(layer, a, 1, c)
                block = jnp.concatenate(
                    [
                        jnp.concatenate([middle, tap(layer, a, 2, c)], axis=1),
                        jnp.concatenate([tap(layer, a, 0, c), middle], axis=1),
                    ],
                    axis=0,
                )
                fore_ref[layer, a, :, c * wide : (c + 1) * wide] = block.astype(jnp.bfloat16)
                if layer:
                    back_ref[layer - 1, 2 - a, :, (2 - c) * wide : (3 - c) * wide] = (
                        block.T.astype(jnp.bfloat16)
                    )

    def convolved(weights, buffer, pair):
        total = None
        for a in range(3):
            columns = pl.ds(pl.multiple_of((2 * pair + a) * X, X), 2 * X)
            term = dot(weights[a], buffer[:, columns])
            total = term if total is None else total + term
        return total

    @pl.loop(0, planes)
    def _(plane):
        both = noise_ref[plane].astype(jnp.float32)
        put(inputs_ref.at[0], plane, jnp.concatenate([both[:, :X], both[:, X:]], axis=0))

    for layer in range(2):

        @pl.loop(0, planes // 2)
        def _(pair):
            total = convolved(fore_ref.at[layer], inputs_ref.at[layer], pair)
            pre_ref[layer, :, pl.ds(pl.multiple_of(2 * pair * X, X), 2 * X)] = total
            act = gelu_of(total)
            put(inputs_ref.at[layer + 1], 2 * pair, act[:, :X])
            put(inputs_ref.at[layer + 1], 2 * pair + 1, act[:, X:])

    critic = jnp.concatenate([disc_ref[4 * a + 2 * b + d] for a in range(2) for d in range(2) for b in range(2)], axis=1)
    critic_back = jnp.concatenate(
        [
            jnp.concatenate(
                [
                    critic[:, (2 * a + d) * wide : (2 * a + d + 1) * wide].astype(jnp.float32).T
                    for d in range(2)
                ],
                axis=1,
            )
            for a in range(2)
        ],
        axis=0,
    ).astype(jnp.bfloat16)
    features = disc_ref.shape[1]
    score = jnp.broadcast_to(score_ref[...], (X, features)).T

    @pl.loop(0, planes // 2)
    def _(pair):
        made = jnp.tanh(convolved(fore_ref.at[2], inputs_ref.at[2], pair))
        rounded = made.astype(jnp.bfloat16)
        exact = rounded.astype(jnp.float32)
        for a in range(2):
            plane = rounded[:, a * X : (a + 1) * X]
            made_all[2 * pair + a, :, 0:X] = plane[:channels]
            made_all[2 * pair + a, :, X : 2 * X] = plane[channels:]
        pieces = []
        for a in range(2):
            plane = exact[:, a * X : (a + 1) * X]
            pieces += [plane, pltpu.roll(plane, X - 1, 1)]
        response = dot(critic, jnp.concatenate(pieces, axis=0).astype(jnp.bfloat16))
        scores = jnp.sum(score * gelu_of(response), axis=0, keepdims=True)
        slope = -jax.nn.sigmoid(-scores)
        upstream = gelu_slope(response) * (slope * score)
        upstream = jnp.where(lax.rem(lane, 2) == 0, upstream, 0.0)
        pieces = jnp.concatenate([upstream, pltpu.roll(upstream, 1, 1)], axis=0)
        spread = dot(critic_back, pieces.astype(jnp.bfloat16))
        for a in range(2):
            plane = made[:, a * X : (a + 1) * X]
            put(grads_ref.at[0], 2 * pair + a, spread[a * wide : (a + 1) * wide] * (1.0 - plane * plane))

    def kernel_sums(layer, gradient):
        for a in range(3):
            sums = dot_rows(gradient, inputs_ref[layer, :, a * X : a * X + cells])
            for c in range(3):
                block = sums[:, c * wide : (c + 1) * wide]
                parts = (
                    block[channels:, :channels],
                    block[:channels, :channels] + block[channels:, channels:],
                    block[:channels, channels:],
                )
                for b in range(3):
                    begin = (27 * layer + 9 * a + 3 * b + c) * channels
                    square_ref[begin : begin + channels, :] = parts[b]

    for layer in (2, 1):
        held = grads_ref.at[2 - layer]
        kernel_sums(layer, held[wide : 2 * wide, X : X + cells])

        @pl.loop(0, planes // 2)
        def _(pair):
            columns = pl.ds(pl.multiple_of(2 * pair * X, X), 2 * X)
            total = convolved(back_ref.at[layer - 1], held, pair)
            total = total * gelu_slope(pre_ref[layer - 1, :, columns])
            if layer == 2:
                put(grads_ref.at[1], 2 * pair, total[:, :X])
                put(grads_ref.at[1], 2 * pair + 1, total[:, X:])
            else:
                later = pl.ds(pl.multiple_of((2 * pair + 1) * X, X), 2 * X)
                grads_ref[0, wide : 2 * wide, later] = total.astype(jnp.bfloat16)

    kernel_sums(0, grads_ref[0, wide : 2 * wide, X : X + cells])

    keep = pick_ref[2] == 1
    place = pick_ref[3]
    own_planes = made_ref.shape[0]
    made_ref[...] = made_all[pl.ds(place * own_planes, own_planes)]
    begin = 2 * place * share_rows
    sums = jnp.concatenate(
        [
            square_ref[pl.ds(begin, share_rows, stride=2), :],
            square_ref[pl.ds(begin + 1, share_rows, stride=2), :],
        ],
        axis=1,
    )
    near_moment = near_moment_ref[...].astype(jnp.float32)[:share_rows]
    near_weight = near_weight_ref[...].astype(jnp.float32)[:share_rows]
    moment = momentum_decay * jnp.where(keep, moment_ref[...], near_moment) + sums
    new_moment_ref[...] = moment
    new_weight_ref[...] = jnp.where(keep, weight_ref[...], near_weight) - step_length * moment


def train(picks, kernels, volume, disc, score, weight, moment, near_weight, near_moment, own):
    planes, channels = volume.shape[0], volume.shape[1]
    wide = 2 * channels
    framed = (planes + 2) * X
    vmem = pl.BlockSpec(memory_space=pltpu.VMEM)
    return pl.pallas_call(
        functools.partial(trainer_kernel, planes),
        out_shape=(
            jax.ShapeDtypeStruct((own,) + volume.shape[1:], jnp.bfloat16),
            jax.ShapeDtypeStruct(weight.shape, jnp.float32),
            jax.ShapeDtypeStruct(weight.shape, jnp.float32),
        ),
        in_specs=[pl.BlockSpec(memory_space=pltpu.SMEM)] + [vmem] * 8,
        out_specs=(vmem,) * 3,
        scratch_shapes=[
            pltpu.VMEM((81 * channels, channels), jnp.float32),
            pltpu.VMEM((3, 3, wide, 3 * wide), jnp.bfloat16),
            pltpu.VMEM((2, 3, wide, 3 * wide), jnp.bfloat16),
            pltpu.VMEM((3, 3 * wide, framed), jnp.bfloat16),
            pltpu.VMEM((2, 3 * wide, framed), jnp.bfloat16),
            pltpu.VMEM((2, wide, planes * X), jnp.float32),
            pltpu.VMEM(volume.shape, jnp.bfloat16),
        ],
        compiler_params=pltpu.CompilerParams(vmem_limit_bytes=VMEM_LIMIT),
    )(picks, kernels, volume, disc, score, weight, moment, near_weight, near_moment)


def on_device(trainers, depth, noise, gen_weight, gen_momentum, disc_weight, score_weight, pairing, flags):
    own = noise.shape[1]
    if own * depth > WHOLE_PLANES or depth < 2 or trainers & (trainers - 1):
        return on_device_split(
            noise, gen_weight, gen_momentum, disc_weight, score_weight, pairing, flags
        )
    rank = lax.axis_index("trainer")
    place = lax.axis_index("depth")
    partner, keeper = pairing[rank], flags[rank]
    apart = jnp.where(keeper == 1, 0, jnp.bitwise_xor(rank, partner))
    picks = []
    for order in bit_orders(trainers):
        picks.append(sum(((apart // bit) % 2) << k for k, bit in enumerate(order)))
    picks = jnp.stack(picks + [keeper, place]).astype(jnp.int32)
    weight, moment = gen_weight.reshape(-1, X), gen_momentum.reshape(-1, X)
    kernels, volume, near_weight, near_moment = exchange(
        trainers, depth, picks, weight, moment, noise[0]
    )
    made, new_weight, new_moment = train(
        picks,
        kernels,
        volume.reshape((own * depth,) + noise.shape[2:]),
        disc_weight[0],
        score_weight,
        weight,
        moment,
        near_weight,
        near_moment,
        own,
    )
    return made[None], new_weight.reshape(gen_weight.shape), new_moment.reshape(gen_weight.shape)


def solution(mesh):
    placed = (
        P("trainer", "depth", None, None),
        P("trainer", "depth"),
        P("trainer", "depth"),
        P("trainer", None, None, None),
        P("trainer", None),
        P(),
        P(),
    )
    return jax.shard_map(
        functools.partial(on_device, mesh.shape["trainer"], mesh.shape["depth"]),
        mesh=mesh,
        in_specs=placed,
        out_specs=(P("trainer", "depth", None, None), P("trainer", "depth"), P("trainer", "depth")),
        check_vma=False,
    )
```

```python
import functools

import jax
import jax.numpy as jnp
from jax import lax
from jax.experimental import pallas as pl
from jax.experimental.pallas import tpu as pltpu
from jax.sharding import PartitionSpec as P

Y = 2
X = 128


momentum_decay = 0.9
step_length = 0.01


def extended(block, sides, width):
    for axis, dim in sides:
        count = lax.axis_size(axis)
        forward = [(i, i + 1) for i in range(count - 1)]
        backward = [(target, source) for source, target in forward]
        low = lax.ppermute(
            lax.slice_in_dim(block, block.shape[dim] - width, None, axis=dim), axis, forward
        )
        high = lax.ppermute(lax.slice_in_dim(block, 0, width, axis=dim), axis, backward)
        block = jnp.concatenate([low, block, high], axis=dim)
    return block


def framed_copies(padded):
    breadth = X
    cells = padded.shape[2]
    framed = jnp.pad(padded, ((0, 0), (0, 0), (breadth + 1, breadth + 1)))
    column = (jnp.arange(cells + 2 * breadth + 2, dtype=jnp.int32) - breadth - 1) % breadth
    left_copy = jnp.where(
        (column == breadth - 1)[None, None, :], jnp.zeros((), framed.dtype), framed
    )
    right_copy = jnp.where((column == 0)[None, None, :], jnp.zeros((), framed.dtype), framed)
    return (left_copy, framed, right_copy)


def stacked_window(copies, read_y, cells):
    breadth = X
    parts_list = []
    for read_x in range(3):
        begin = read_y * breadth + read_x
        parts_list.append(copies[read_x][:, :, begin : begin + cells])
    return jnp.concatenate(parts_list, axis=1)


def group_kernel(layer):
    channels = layer.shape[-1]
    cube = layer.reshape(3, 3, 3, channels, channels)
    return cube.transpose(0, 1, 3, 2, 4).reshape(3, 3, channels, 3 * channels)


def flip_kernel(layer):
    channels = layer.shape[-1]
    cube = layer.reshape(3, 3, 3, channels, channels)[::-1, ::-1, ::-1].swapaxes(3, 4)
    return cube.transpose(0, 1, 3, 2, 4).reshape(3, 3, channels, 3 * channels)


def convolve_grouped(padded, grouped):
    planes, cells = (padded.shape[0] - 2, padded.shape[2])
    copies = framed_copies(padded)
    summed = jnp.zeros((planes, grouped.shape[2], cells), jnp.float32)
    for read_y in range(3):
        window = stacked_window(copies, read_y, cells)
        for read_z in range(3):
            summed = summed + jnp.einsum(
                "oj,zjs->zos",
                grouped[read_z, read_y],
                window[read_z : read_z + planes],
                preferred_element_type=jnp.float32,
            )
    return summed


def convolve(padded, layer):
    return convolve_grouped(padded, group_kernel(layer))


def convolve_back(padded, layer):
    return convolve_grouped(padded, flip_kernel(layer))


def kernel_grad(gradient, padded):
    planes, channels_out, cells = gradient.shape
    channels_in = padded.shape[1]
    copies = framed_copies(padded)
    rows_list = []
    for read_z in range(3):
        row_list = []
        for read_y in range(3):
            window = stacked_window(copies, read_y, cells)
            row_list.append(
                jnp.einsum(
                    "zos,zjs->oj",
                    gradient,
                    window[read_z : read_z + planes],
                    preferred_element_type=jnp.float32,
                )
            )
        rows_list.append(jnp.stack(row_list))
    grouped = jnp.stack(rows_list)
    return (
        grouped.reshape(3, 3, channels_out, 3, channels_in)
        .transpose(0, 1, 3, 2, 4)
        .reshape(27, channels_out, channels_in)
    )


def gelu_back(inputs, upstream):
    return jax.vjp(jax.nn.gelu, inputs)[1](upstream)[0]


def widen_back(gradient):
    return extended(gradient, (("depth", 0),), 1)


def widen_forward(volume):
    return extended(volume, (("depth", 0),), 1)


def critic_grad(generated, disc_kernel, score_vector):
    planes, channels, cells = generated.shape
    blocks = generated.reshape(planes // 2, 2, channels, Y // 2, 2, X // 2, 2)
    kernel_cube = disc_kernel.reshape(2, 2, 2, disc_kernel.shape[1], channels)
    response = jnp.einsum(
        "abdoc,zacybxd->zoyx", kernel_cube, blocks, preferred_element_type=jnp.float32
    )
    features = jax.nn.gelu(response)
    scores = jnp.sum(score_vector[None, :, None, None] * features, axis=1)
    slope = -jax.nn.sigmoid(-scores)
    upstream = gelu_back(response, slope[:, None] * score_vector[None, :, None, None]).astype(
        jnp.bfloat16
    )
    spread = jnp.einsum(
        "abdoc,zoyx->zacybxd", kernel_cube, upstream, preferred_element_type=jnp.float32
    )
    return spread.reshape(planes, channels, cells)


def on_device_split(noise, gen_weight, gen_momentum, disc_weight, score_weight, pairing, flags):
    trainer_rank = lax.axis_index("trainer")
    partner = pairing[trainer_rank]
    keeper = flags[trainer_rank] == 1
    trainer_count = lax.axis_size("trainer")
    own_pair = jnp.concatenate([gen_weight, gen_momentum], axis=0)
    slot_ids = jnp.arange(trainer_count, dtype=jnp.int32)
    outgoing = jnp.where((slot_ids == partner)[:, None, None], own_pair[None], 0.0)
    incoming = lax.all_to_all(
        outgoing.astype(jnp.bfloat16), "trainer", split_axis=0, concat_axis=0, tiled=True
    ).astype(outgoing.dtype)
    arrived = lax.dynamic_index_in_dim(incoming, partner, 0, keepdims=False)
    other_weight, other_moment = (arrived[0:1], arrived[1:2])
    chosen_weight = jnp.where(keeper, gen_weight, other_weight)
    chosen_momentum = jnp.where(keeper, gen_momentum, other_moment)
    channels = noise.shape[2]
    all_kernels = lax.all_gather(chosen_weight.astype(jnp.bfloat16), "depth", axis=1, tiled=True)
    layers = all_kernels.reshape(3, 27, channels, channels)
    latent = noise[0]
    latent_pad = widen_forward(latent)
    first_pre = convolve(latent_pad, layers[0])
    first_act_pad = widen_forward(jax.nn.gelu(first_pre).astype(jnp.bfloat16))
    second_pre = convolve(first_act_pad, layers[1])
    second_act_pad = widen_forward(jax.nn.gelu(second_pre).astype(jnp.bfloat16))
    third_pre = convolve(second_act_pad, layers[2])
    output_f = jnp.tanh(third_pre)
    generated = output_f.astype(jnp.bfloat16)
    gen_grad = critic_grad(generated, disc_weight[0], score_weight[0])
    third_grad = (gen_grad * (1.0 - output_f * output_f)).astype(jnp.bfloat16)
    grad_three = kernel_grad(third_grad, second_act_pad)
    second_back = convolve_back(widen_back(third_grad), layers[2])
    second_grad = gelu_back(second_pre, second_back).astype(jnp.bfloat16)
    grad_two = kernel_grad(second_grad, first_act_pad)
    first_back = convolve_back(widen_back(second_grad), layers[1])
    first_grad = gelu_back(first_pre, first_back).astype(jnp.bfloat16)
    grad_one = kernel_grad(first_grad, latent_pad)
    local_grad = jnp.concatenate(
        [grad_one.reshape(-1), grad_two.reshape(-1), grad_three.reshape(-1)]
    )
    share_len = gen_weight.shape[1]
    grad_whole = lax.psum(local_grad.astype(jnp.bfloat16), "depth").astype(jnp.float32)
    grad_share = lax.dynamic_slice_in_dim(
        grad_whole, lax.axis_index("depth") * share_len, share_len, 0
    )
    new_momentum = momentum_decay * chosen_momentum + grad_share[None, :]
    new_weight = chosen_weight - step_length * new_momentum
    return (generated[None], new_weight, new_momentum)


MESH = pl.DeviceIdType.MESH
VMEM_LIMIT = 56 * 1024 * 1024
WHOLE_PLANES = 16


def bit_orders(count):
    bits = [1 << k for k in range(count.bit_length() - 1)]
    return bits[1:] + bits[:1], bits[:0:-1] + bits[:1]


def flipped(index, bit):
    return index + bit - 2 * bit * lax.rem(index // bit, 2)


def doubling(slots, order, rank, send_sem, recv_sem):
    for k, bit in enumerate(order):
        copy = pltpu.make_async_remote_copy(
            src_ref=slots.at[pl.ds(0, 1 << k)],
            dst_ref=slots.at[pl.ds(1 << k, 1 << k)],
            send_sem=send_sem.at[k],
            recv_sem=recv_sem.at[k],
            device_id={"trainer": flipped(rank, bit)},
            device_id_type=MESH,
        )
        copy.start()
        yield
        copy.wait()


def line_gather(slots, place, count, up_send, up_recv, down_send, down_recv):
    def move(slot, target, send_sem, recv_sem):
        return pltpu.make_async_remote_copy(
            src_ref=slots.at[slot],
            dst_ref=slots.at[slot],
            send_sem=send_sem,
            recv_sem=recv_sem,
            device_id={"depth": target},
            device_id_type=MESH,
        )

    def up(step):
        return move(jnp.maximum(place - step, 0), place + 1, up_send.at[step], up_recv.at[step])

    def down(step):
        return move(
            jnp.minimum(place + step, count - 1), place - 1, down_send.at[step], down_recv.at[step]
        )

    for step in range(count - 1):

        @pl.when((place < count - 1) & (place >= step))
        def _():
            up(step).start()

        @pl.when((place > 0) & (place + step <= count - 1))
        def _():
            down(step).start()

        yield

        @pl.when(place >= step + 1)
        def _():
            up(step).wait_recv()

        @pl.when(place + step + 1 <= count - 1)
        def _():
            down(step).wait_recv()

    yield
    for step in range(count - 1):

        @pl.when((place < count - 1) & (place >= step))
        def _():
            up(step).wait_send()

        @pl.when((place > 0) & (place + step <= count - 1))
        def _():
            down(step).wait_send()


def advance(*steps):
    alive = False
    for each in steps:
        alive = next(each, 0) is None or alive
    return alive


ROOT = 0.7978845608028654
CUBIC = 0.044715


def gelu_of(inputs):
    bend = jnp.tanh(ROOT * (inputs + CUBIC * (inputs * inputs * inputs)))
    return 0.5 * inputs * (1.0 + bend)


def gelu_slope(inputs):
    square = inputs * inputs
    bend = jnp.tanh(ROOT * (inputs + CUBIC * (square * inputs)))
    tilt = ROOT * (1.0 + 3.0 * CUBIC * square)
    return 0.5 * (1.0 + bend) + 0.5 * inputs * (1.0 - bend * bend) * tilt


def dot(left, right):
    return jnp.dot(left, right, preferred_element_type=jnp.float32)


def dot_rows(left, right):
    return lax.dot_general(
        left, right, (((1,), (1,)), ((), ())), preferred_element_type=jnp.float32
    )


def round_kernel(
    trainers,
    depth,
    pairing_ref,
    flags_ref,
    weight_ref,
    moment_ref,
    noise_ref,
    disc_ref,
    score_ref,
    made_ref,
    new_weight_ref,
    new_moment_ref,
    kernels_ref,
    volume_ref,
    weight_a,
    weight_b,
    moment_a,
    moment_b,
    square_ref,
    fore_ref,
    back_ref,
    inputs_ref,
    grads_ref,
    pre_ref,
    made_all,
    critic_ref,
    critic_back_ref,
    send_sem,
    recv_sem,
    line_sem,
):
    own, channels = noise_ref.shape[0], noise_ref.shape[1]
    planes = own * depth
    wide = 2 * channels
    cells = planes * X
    share_rows = weight_ref.shape[0]
    rank = lax.axis_index("trainer")
    place = lax.axis_index("depth")
    order_a, order_b = bit_orders(trainers)
    barrier = pltpu.get_barrier_semaphore()
    for bit in order_a:
        pl.semaphore_signal(
            barrier, inc=1, device_id={"trainer": flipped(rank, bit)}, device_id_type=MESH
        )

    @pl.when(place > 0)
    def _():
        pl.semaphore_signal(barrier, inc=1, device_id={"depth": place - 1}, device_id_type=MESH)

    @pl.when(place < depth - 1)
    def _():
        pl.semaphore_signal(barrier, inc=1, device_id={"depth": place + 1}, device_id_type=MESH)

    half = weight_a.shape[1]
    padding = jnp.zeros((2 * half - share_rows, weight_ref.shape[1]), jnp.float32)
    weight_a[0] = weight_ref[:half].astype(jnp.bfloat16)
    weight_b[0] = jnp.concatenate([weight_ref[half:], padding], axis=0).astype(jnp.bfloat16)
    moment_a[0] = moment_ref[:half].astype(jnp.bfloat16)
    moment_b[0] = jnp.concatenate([moment_ref[half:], padding], axis=0).astype(jnp.bfloat16)
    volume_ref[place] = noise_ref[...]

    beside = (place > 0).astype(jnp.int32) + (place < depth - 1).astype(jnp.int32)
    pl.semaphore_wait(barrier, len(order_a) + beside)

    noise_line = line_gather(
        volume_ref, place, depth, line_sem.at[0], line_sem.at[1], line_sem.at[2], line_sem.at[3]
    )
    first = doubling(weight_a, order_a, rank, send_sem.at[0], recv_sem.at[0])
    second = doubling(weight_b, order_b, rank, send_sem.at[1], recv_sem.at[1])
    third = doubling(moment_a, order_a, rank, send_sem.at[2], recv_sem.at[2])
    fourth = doubling(moment_b, order_b, rank, send_sem.at[3], recv_sem.at[3])
    share_line = line_gather(
        kernels_ref, place, depth, line_sem.at[4], line_sem.at[5], line_sem.at[6], line_sem.at[7]
    )
    advance(first, second, noise_line)

    lane = lax.broadcasted_iota(jnp.int32, (wide, X), 1)
    blocks = [
        [jnp.concatenate([disc_ref[4 * a + 2 * b + d] for b in range(2)], axis=0) for d in range(2)]
        for a in range(2)
    ]
    for a in range(2):
        for d in range(2):
            at = 2 * a + d
            critic_back_ref[a * wide : (a + 1) * wide, d * X : (d + 1) * X] = blocks[a][d]
            critic_ref[:, at * wide : (at + 1) * wide] = (
                blocks[a][d].astype(jnp.float32).T.astype(jnp.bfloat16)
            )
    empty = jnp.zeros((3 * wide, X), jnp.bfloat16)
    for buffer in [inputs_ref.at[k] for k in range(3)] + [grads_ref.at[k] for k in range(2)]:
        buffer[:, 0:X] = empty
        buffer[:, cells + X : cells + 2 * X] = empty

    while advance(first, second):
        advance(noise_line)

    keep = flags_ref[rank] == 1
    partner = pairing_ref[rank]
    picks = []
    for order in (order_a, order_b):
        pick = 0
        for k, bit in enumerate(order):
            differs = lax.rem(rank // bit + partner // bit, 2)
            pick = pick + differs * (1 << k)
        picks.append(jnp.where(keep, 0, pick))
    kernels_ref[place, :half] = weight_a[picks[0]]
    kernels_ref[place, half:] = weight_b[picks[1]]
    advance(share_line, third, fourth)

    def put(buffer, plane, value):
        columns = pl.ds(pl.multiple_of((plane + 1) * X, X), X)
        low = jnp.where(lane == 0, 0.0, pltpu.roll(value, 1, 1))
        high = jnp.where(lane == X - 1, 0.0, pltpu.roll(value, X - 1, 1))
        buffer[0:wide, columns] = low.astype(jnp.bfloat16)
        buffer[wide : 2 * wide, columns] = value.astype(jnp.bfloat16)
        buffer[2 * wide : 3 * wide, columns] = high.astype(jnp.bfloat16)

    def unpack(part):
        rows = kernels_ref[part].astype(jnp.float32)[:share_rows]
        begin = pl.multiple_of(2 * part * share_rows, 8)
        square_ref[pl.ds(begin, share_rows, stride=2), :] = rows[:, :channels]
        square_ref[pl.ds(begin + 1, share_rows, stride=2), :] = rows[:, channels:]

    def tap(layer, a, b, c):
        begin = (27 * layer + 9 * a + 3 * b + c) * channels
        return square_ref[begin : begin + channels, :]

    def prepare(layer):
        for a in range(3):
            for c in range(3):
                middle = tap(layer, a, 1, c)
                block = jnp.concatenate(
                    [
                        jnp.concatenate([middle, tap(layer, a, 2, c)], axis=1),
                        jnp.concatenate([tap(layer, a, 0, c), middle], axis=1),
                    ],
                    axis=0,
                )
                fore_ref[layer, a, :, c * wide : (c + 1) * wide] = block.astype(jnp.bfloat16)
                if layer:
                    back_ref[layer - 1, 2 - a, :, (2 - c) * wide : (3 - c) * wide] = (
                        block.T.astype(jnp.bfloat16)
                    )

    def convolved(weights, buffer, pair):
        total = None
        for a in range(3):
            columns = pl.ds(pl.multiple_of((2 * pair + a) * X, X), 2 * X)
            term = dot(weights[a], buffer[:, columns])
            total = term if total is None else total + term
        return total

    def forward(layer):
        prepare(layer)

        @pl.loop(0, planes // 2)
        def _(pair):
            total = convolved(fore_ref.at[layer], inputs_ref.at[layer], pair)
            if layer < 2:
                pre_ref[layer, :, pl.ds(pl.multiple_of(2 * pair * X, X), 2 * X)] = total
                act = gelu_of(total)
                put(inputs_ref.at[layer + 1], 2 * pair, act[:, :X])
                put(inputs_ref.at[layer + 1], 2 * pair + 1, act[:, X:])
            else:
                criticise(pair, jnp.tanh(total))

    score = jnp.broadcast_to(score_ref[...], (X, X)).T

    def criticise(pair, made):
        rounded = made.astype(jnp.bfloat16)
        exact = rounded.astype(jnp.float32)
        for a in range(2):
            plane = rounded[:, a * X : (a + 1) * X]
            made_all[2 * pair + a, :, 0:X] = plane[:channels]
            made_all[2 * pair + a, :, X : 2 * X] = plane[channels:]
        pieces = []
        for a in range(2):
            plane = exact[:, a * X : (a + 1) * X]
            pieces += [plane, pltpu.roll(plane, X - 1, 1)]
        response = dot(critic_ref[...], jnp.concatenate(pieces, axis=0).astype(jnp.bfloat16))
        scores = jnp.sum(score * gelu_of(response), axis=0, keepdims=True)
        slope = -jax.nn.sigmoid(-scores)
        upstream = gelu_slope(response) * (slope * score)
        upstream = jnp.where(lax.rem(lane, 2) == 0, upstream, 0.0)
        pieces = jnp.concatenate([upstream, pltpu.roll(upstream, 1, 1)], axis=0)
        spread = dot(critic_back_ref[...], pieces.astype(jnp.bfloat16))
        for a in range(2):
            plane = made[:, a * X : (a + 1) * X]
            fall = 1.0 - plane * plane
            put(grads_ref.at[0], 2 * pair + a, spread[a * wide : (a + 1) * wide] * fall)

    unpack(place)
    while advance(noise_line):
        pass
    for part in range(depth):

        @pl.loop(0, own)
        def _(plane):
            both = volume_ref[part, plane].astype(jnp.float32)
            whole = jnp.concatenate([both[:, :X], both[:, X:]], axis=0)
            put(inputs_ref.at[0], part * own + plane, whole)

    layer_rows = 27 * channels
    edges = []
    for layer in range(3):
        edges.append((layer * layer_rows // (2 * share_rows), ((layer + 1) * layer_rows - 1) // (2 * share_rows)))

    def ready(layer, at):
        return max(abs(edge - at) for edges_of in edges[: layer + 1] for edge in edges_of)

    for step in range(depth):
        if step:
            advance(share_line)
            advance(third, fourth)

            @pl.when(place >= step)
            def _():
                unpack(place - step)

            @pl.when(place + step <= depth - 1)
            def _():
                unpack(place + step)

        for layer in range(3):
            places = [at for at in range(depth) if ready(layer, at) == step]
            if places:
                here = place == places[0]
                for at in places[1:]:
                    here = here | (place == at)

                @pl.when(here)
                def _():
                    forward(layer)

    begin = 2 * place * share_rows

    def kernel_sums(layer, gradient):
        for a in range(3):
            low = (27 * layer + 9 * a) * channels

            @pl.when((low + 9 * channels > begin) & (low < begin + 2 * share_rows))
            def _():
                sums = dot_rows(gradient[...], inputs_ref[layer, :, a * X : a * X + cells])
                for c in range(3):
                    block = sums[:, c * wide : (c + 1) * wide]
                    parts = (
                        block[channels:, :channels],
                        block[:channels, :channels] + block[channels:, channels:],
                        block[:channels, channels:],
                    )
                    for b in range(3):
                        row = low + (3 * b + c) * channels
                        square_ref[row : row + channels, :] = parts[b]

    for layer in (2, 1):
        held = grads_ref.at[2 - layer]
        kernel_sums(layer, held.at[wide : 2 * wide, X : X + cells])

        @pl.when(begin < layer * layer_rows)
        def _():
            @pl.loop(0, planes // 2)
            def _(pair):
                columns = pl.ds(pl.multiple_of(2 * pair * X, X), 2 * X)
                total = convolved(back_ref.at[layer - 1], held, pair)
                total = total * gelu_slope(pre_ref[layer - 1, :, columns])
                if layer == 2:
                    put(grads_ref.at[1], 2 * pair, total[:, :X])
                    put(grads_ref.at[1], 2 * pair + 1, total[:, X:])
                else:
                    later = pl.ds(pl.multiple_of((2 * pair + 1) * X, X), 2 * X)
                    grads_ref[0, wide : 2 * wide, later] = total.astype(jnp.bfloat16)

    kernel_sums(0, grads_ref.at[0, wide : 2 * wide, X : X + cells])

    while advance(share_line, third, fourth):
        pass
    made_ref[...] = made_all[pl.ds(place * own, own)]
    sums = jnp.concatenate(
        [
            square_ref[pl.ds(begin, share_rows, stride=2), :],
            square_ref[pl.ds(begin + 1, share_rows, stride=2), :],
        ],
        axis=1,
    )

    def adopted(mine, near):
        return jnp.where(keep, mine, near.astype(jnp.float32)[:share_rows])

    near = jnp.concatenate([moment_a[picks[0]], moment_b[picks[1]]], axis=0)
    moment = momentum_decay * adopted(moment_ref[...], near) + sums
    new_moment_ref[...] = moment
    new_weight_ref[...] = adopted(weight_ref[...], kernels_ref[place]) - step_length * moment


def on_device(trainers, depth, noise, gen_weight, gen_momentum, disc_weight, score_weight, pairing, flags):
    own, channels = noise.shape[1], noise.shape[2]
    planes = own * depth
    if planes > WHOLE_PLANES or depth < 2 or trainers & (trainers - 1):
        return on_device_split(
            noise, gen_weight, gen_momentum, disc_weight, score_weight, pairing, flags
        )
    weight, moment = gen_weight.reshape(-1, X), gen_momentum.reshape(-1, X)
    rows = weight.shape[0]
    half = -(-rows // 32) * 16
    levels = trainers.bit_length() - 1
    wide = 2 * channels
    framed = (planes + 2) * X
    vmem = pl.BlockSpec(memory_space=pltpu.VMEM)
    smem = pl.BlockSpec(memory_space=pltpu.SMEM)
    slots = pltpu.VMEM((trainers, half, X), jnp.bfloat16)
    made, new_weight, new_moment = pl.pallas_call(
        functools.partial(round_kernel, trainers, depth),
        out_shape=(
            jax.ShapeDtypeStruct(noise.shape[1:], jnp.bfloat16),
            jax.ShapeDtypeStruct(weight.shape, jnp.float32),
            jax.ShapeDtypeStruct(weight.shape, jnp.float32),
        ),
        in_specs=[smem] * 2 + [vmem] * 5,
        out_specs=(vmem,) * 3,
        scratch_shapes=[
            pltpu.VMEM((depth, 2 * half, X), jnp.bfloat16),
            pltpu.VMEM((depth,) + noise.shape[1:], jnp.bfloat16),
            slots,
            slots,
            slots,
            slots,
            pltpu.VMEM((81 * channels, channels), jnp.float32),
            pltpu.VMEM((3, 3, wide, 3 * wide), jnp.bfloat16),
            pltpu.VMEM((2, 3, wide, 3 * wide), jnp.bfloat16),
            pltpu.VMEM((3, 3 * wide, framed), jnp.bfloat16),
            pltpu.VMEM((2, 3 * wide, framed), jnp.bfloat16),
            pltpu.VMEM((2, wide, planes * X), jnp.float32),
            pltpu.VMEM((planes,) + noise.shape[2:], jnp.bfloat16),
            pltpu.VMEM((X, 4 * wide), jnp.bfloat16),
            pltpu.VMEM((2 * wide, 2 * X), jnp.bfloat16),
            pltpu.SemaphoreType.DMA((4, levels)),
            pltpu.SemaphoreType.DMA((4, levels)),
            pltpu.SemaphoreType.DMA((8, depth - 1)),
        ],
        compiler_params=pltpu.CompilerParams(
            collective_id=0, has_side_effects=True, vmem_limit_bytes=VMEM_LIMIT
        ),
    )(
        pairing,
        flags,
        weight,
        moment,
        noise[0],
        disc_weight[0].swapaxes(1, 2),
        score_weight,
    )
    return made[None], new_weight.reshape(gen_weight.shape), new_moment.reshape(gen_weight.shape)


def solution(mesh):
    placed = (
        P("trainer", "depth", None, None),
        P("trainer", "depth"),
        P("trainer", "depth"),
        P("trainer", None, None, None),
        P("trainer", None),
        P(),
        P(),
    )
    return jax.shard_map(
        functools.partial(on_device, mesh.shape["trainer"], mesh.shape["depth"]),
        mesh=mesh,
        in_specs=placed,
        out_specs=(P("trainer", "depth", None, None), P("trainer", "depth"), P("trainer", "depth")),
        check_vma=False,
    )
```

```python
import functools

import jax
import jax.numpy as jnp
from jax import lax
from jax.experimental import pallas as pl
from jax.experimental.pallas import tpu as pltpu
from jax.sharding import PartitionSpec as P

Y = 2
X = 128


momentum_decay = 0.9
step_length = 0.01


def extended(block, sides, width):
    for axis, dim in sides:
        count = lax.axis_size(axis)
        forward = [(i, i + 1) for i in range(count - 1)]
        backward = [(target, source) for source, target in forward]
        low = lax.ppermute(
            lax.slice_in_dim(block, block.shape[dim] - width, None, axis=dim), axis, forward
        )
        high = lax.ppermute(lax.slice_in_dim(block, 0, width, axis=dim), axis, backward)
        block = jnp.concatenate([low, block, high], axis=dim)
    return block


def framed_copies(padded):
    breadth = X
    cells = padded.shape[2]
    framed = jnp.pad(padded, ((0, 0), (0, 0), (breadth + 1, breadth + 1)))
    column = (jnp.arange(cells + 2 * breadth + 2, dtype=jnp.int32) - breadth - 1) % breadth
    left_copy = jnp.where(
        (column == breadth - 1)[None, None, :], jnp.zeros((), framed.dtype), framed
    )
    right_copy = jnp.where((column == 0)[None, None, :], jnp.zeros((), framed.dtype), framed)
    return (left_copy, framed, right_copy)


def stacked_window(copies, read_y, cells):
    breadth = X
    parts_list = []
    for read_x in range(3):
        begin = read_y * breadth + read_x
        parts_list.append(copies[read_x][:, :, begin : begin + cells])
    return jnp.concatenate(parts_list, axis=1)


def group_kernel(layer):
    channels = layer.shape[-1]
    cube = layer.reshape(3, 3, 3, channels, channels)
    return cube.transpose(0, 1, 3, 2, 4).reshape(3, 3, channels, 3 * channels)


def flip_kernel(layer):
    channels = layer.shape[-1]
    cube = layer.reshape(3, 3, 3, channels, channels)[::-1, ::-1, ::-1].swapaxes(3, 4)
    return cube.transpose(0, 1, 3, 2, 4).reshape(3, 3, channels, 3 * channels)


def convolve_grouped(padded, grouped):
    planes, cells = (padded.shape[0] - 2, padded.shape[2])
    copies = framed_copies(padded)
    summed = jnp.zeros((planes, grouped.shape[2], cells), jnp.float32)
    for read_y in range(3):
        window = stacked_window(copies, read_y, cells)
        for read_z in range(3):
            summed = summed + jnp.einsum(
                "oj,zjs->zos",
                grouped[read_z, read_y],
                window[read_z : read_z + planes],
                preferred_element_type=jnp.float32,
            )
    return summed


def convolve(padded, layer):
    return convolve_grouped(padded, group_kernel(layer))


def convolve_back(padded, layer):
    return convolve_grouped(padded, flip_kernel(layer))


def kernel_grad(gradient, padded):
    planes, channels_out, cells = gradient.shape
    channels_in = padded.shape[1]
    copies = framed_copies(padded)
    rows_list = []
    for read_z in range(3):
        row_list = []
        for read_y in range(3):
            window = stacked_window(copies, read_y, cells)
            row_list.append(
                jnp.einsum(
                    "zos,zjs->oj",
                    gradient,
                    window[read_z : read_z + planes],
                    preferred_element_type=jnp.float32,
                )
            )
        rows_list.append(jnp.stack(row_list))
    grouped = jnp.stack(rows_list)
    return (
        grouped.reshape(3, 3, channels_out, 3, channels_in)
        .transpose(0, 1, 3, 2, 4)
        .reshape(27, channels_out, channels_in)
    )


def gelu_back(inputs, upstream):
    return jax.vjp(jax.nn.gelu, inputs)[1](upstream)[0]


def widen_back(gradient):
    return extended(gradient, (("depth", 0),), 1)


def widen_forward(volume):
    return extended(volume, (("depth", 0),), 1)


def critic_grad(generated, disc_kernel, score_vector):
    planes, channels, cells = generated.shape
    blocks = generated.reshape(planes // 2, 2, channels, Y // 2, 2, X // 2, 2)
    kernel_cube = disc_kernel.reshape(2, 2, 2, disc_kernel.shape[1], channels)
    response = jnp.einsum(
        "abdoc,zacybxd->zoyx", kernel_cube, blocks, preferred_element_type=jnp.float32
    )
    features = jax.nn.gelu(response)
    scores = jnp.sum(score_vector[None, :, None, None] * features, axis=1)
    slope = -jax.nn.sigmoid(-scores)
    upstream = gelu_back(response, slope[:, None] * score_vector[None, :, None, None]).astype(
        jnp.bfloat16
    )
    spread = jnp.einsum(
        "abdoc,zoyx->zacybxd", kernel_cube, upstream, preferred_element_type=jnp.float32
    )
    return spread.reshape(planes, channels, cells)


def on_device_split(noise, gen_weight, gen_momentum, disc_weight, score_weight, pairing, flags):
    trainer_rank = lax.axis_index("trainer")
    partner = pairing[trainer_rank]
    keeper = flags[trainer_rank] == 1
    trainer_count = lax.axis_size("trainer")
    own_pair = jnp.concatenate([gen_weight, gen_momentum], axis=0)
    slot_ids = jnp.arange(trainer_count, dtype=jnp.int32)
    outgoing = jnp.where((slot_ids == partner)[:, None, None], own_pair[None], 0.0)
    incoming = lax.all_to_all(
        outgoing.astype(jnp.bfloat16), "trainer", split_axis=0, concat_axis=0, tiled=True
    ).astype(outgoing.dtype)
    arrived = lax.dynamic_index_in_dim(incoming, partner, 0, keepdims=False)
    other_weight, other_moment = (arrived[0:1], arrived[1:2])
    chosen_weight = jnp.where(keeper, gen_weight, other_weight)
    chosen_momentum = jnp.where(keeper, gen_momentum, other_moment)
    channels = noise.shape[2]
    all_kernels = lax.all_gather(chosen_weight.astype(jnp.bfloat16), "depth", axis=1, tiled=True)
    layers = all_kernels.reshape(3, 27, channels, channels)
    latent = noise[0]
    latent_pad = widen_forward(latent)
    first_pre = convolve(latent_pad, layers[0])
    first_act_pad = widen_forward(jax.nn.gelu(first_pre).astype(jnp.bfloat16))
    second_pre = convolve(first_act_pad, layers[1])
    second_act_pad = widen_forward(jax.nn.gelu(second_pre).astype(jnp.bfloat16))
    third_pre = convolve(second_act_pad, layers[2])
    output_f = jnp.tanh(third_pre)
    generated = output_f.astype(jnp.bfloat16)
    gen_grad = critic_grad(generated, disc_weight[0], score_weight[0])
    third_grad = (gen_grad * (1.0 - output_f * output_f)).astype(jnp.bfloat16)
    grad_three = kernel_grad(third_grad, second_act_pad)
    second_back = convolve_back(widen_back(third_grad), layers[2])
    second_grad = gelu_back(second_pre, second_back).astype(jnp.bfloat16)
    grad_two = kernel_grad(second_grad, first_act_pad)
    first_back = convolve_back(widen_back(second_grad), layers[1])
    first_grad = gelu_back(first_pre, first_back).astype(jnp.bfloat16)
    grad_one = kernel_grad(first_grad, latent_pad)
    local_grad = jnp.concatenate(
        [grad_one.reshape(-1), grad_two.reshape(-1), grad_three.reshape(-1)]
    )
    share_len = gen_weight.shape[1]
    grad_whole = lax.psum(local_grad.astype(jnp.bfloat16), "depth").astype(jnp.float32)
    grad_share = lax.dynamic_slice_in_dim(
        grad_whole, lax.axis_index("depth") * share_len, share_len, 0
    )
    new_momentum = momentum_decay * chosen_momentum + grad_share[None, :]
    new_weight = chosen_weight - step_length * new_momentum
    return (generated[None], new_weight, new_momentum)


MESH = pl.DeviceIdType.MESH
VMEM_LIMIT = 32 * 1024 * 1024
WHOLE_PLANES = 16


def bit_orders(count):
    bits = [1 << k for k in range(count.bit_length() - 1)]
    return bits[1:] + bits[:1], bits[:0:-1] + bits[:1]


def flipped(index, bit):
    return index + bit - 2 * bit * lax.rem(index // bit, 2)


def doubling(slots, order, rank, send_sem, recv_sem):
    for k, bit in enumerate(order):
        copy = pltpu.make_async_remote_copy(
            src_ref=slots.at[pl.ds(0, 1 << k)],
            dst_ref=slots.at[pl.ds(1 << k, 1 << k)],
            send_sem=send_sem.at[k],
            recv_sem=recv_sem.at[k],
            device_id={"trainer": flipped(rank, bit)},
            device_id_type=MESH,
        )
        copy.start()
        yield
        copy.wait()


def line_gather(slots, place, count, up_send, up_recv, down_send, down_recv):
    def move(slot, target, send_sem, recv_sem):
        return pltpu.make_async_remote_copy(
            src_ref=slots.at[slot],
            dst_ref=slots.at[slot],
            send_sem=send_sem,
            recv_sem=recv_sem,
            device_id={"depth": target},
            device_id_type=MESH,
        )

    def up(step):
        return move(jnp.maximum(place - step, 0), place + 1, up_send.at[step], up_recv.at[step])

    def down(step):
        return move(
            jnp.minimum(place + step, count - 1), place - 1, down_send.at[step], down_recv.at[step]
        )

    for step in range(count - 1):

        @pl.when((place < count - 1) & (place >= step))
        def _():
            up(step).start()

        @pl.when((place > 0) & (place + step <= count - 1))
        def _():
            down(step).start()

        yield

        @pl.when(place >= step + 1)
        def _():
            up(step).wait_recv()

        @pl.when(place + step + 1 <= count - 1)
        def _():
            down(step).wait_recv()

    yield
    for step in range(count - 1):

        @pl.when((place < count - 1) & (place >= step))
        def _():
            up(step).wait_send()

        @pl.when((place > 0) & (place + step <= count - 1))
        def _():
            down(step).wait_send()


def advance(*steps):
    alive = False
    for each in steps:
        alive = next(each, 0) is None or alive
    return alive


ROOT = 0.7978845608028654
CUBIC = 0.044715


def gelu_of(inputs):
    bend = jnp.tanh(ROOT * (inputs + CUBIC * (inputs * inputs * inputs)))
    return 0.5 * inputs * (1.0 + bend)


def gelu_slope(inputs):
    square = inputs * inputs
    bend = jnp.tanh(ROOT * (inputs + CUBIC * (square * inputs)))
    tilt = ROOT * (1.0 + 3.0 * CUBIC * square)
    return 0.5 * (1.0 + bend) + 0.5 * inputs * (1.0 - bend * bend) * tilt


def dot(left, right):
    return jnp.dot(left, right, preferred_element_type=jnp.float32)


def dot_rows(left, right):
    return lax.dot_general(
        left, right, (((1,), (1,)), ((), ())), preferred_element_type=jnp.float32
    )


def round_kernel(
    trainers,
    depth,
    pairing_ref,
    flags_ref,
    weight_ref,
    moment_ref,
    noise_ref,
    disc_ref,
    score_ref,
    made_ref,
    new_weight_ref,
    new_moment_ref,
    kernels_a,
    kernels_b,
    volume_ref,
    weight_a,
    weight_b,
    moment_a,
    moment_b,
    square_ref,
    fore_ref,
    back_ref,
    inputs_ref,
    grads_ref,
    pre_ref,
    made_all,
    critic_ref,
    critic_back_ref,
    send_sem,
    recv_sem,
    line_sem,
):
    own, channels = noise_ref.shape[0], noise_ref.shape[1]
    planes = own * depth
    wide = 2 * channels
    cells = planes * X
    share_rows = weight_ref.shape[0]
    rank = lax.axis_index("trainer")
    place = lax.axis_index("depth")
    order_a, order_b = bit_orders(trainers)
    barrier = pltpu.get_barrier_semaphore()
    for bit in order_a:
        pl.semaphore_signal(
            barrier, inc=1, device_id={"trainer": flipped(rank, bit)}, device_id_type=MESH
        )

    @pl.when(place > 0)
    def _():
        pl.semaphore_signal(barrier, inc=1, device_id={"depth": place - 1}, device_id_type=MESH)

    @pl.when(place < depth - 1)
    def _():
        pl.semaphore_signal(barrier, inc=1, device_id={"depth": place + 1}, device_id_type=MESH)

    half = weight_a.shape[1]
    padding = jnp.zeros((2 * half - share_rows, weight_ref.shape[1]), jnp.float32)
    weight_a[0] = weight_ref[:half].astype(jnp.bfloat16)
    weight_b[0] = jnp.concatenate([weight_ref[half:], padding], axis=0).astype(jnp.bfloat16)
    moment_a[0] = moment_ref[:half].astype(jnp.bfloat16)
    moment_b[0] = jnp.concatenate([moment_ref[half:], padding], axis=0).astype(jnp.bfloat16)
    volume_ref[place] = noise_ref[...]

    beside = (place > 0).astype(jnp.int32) + (place < depth - 1).astype(jnp.int32)
    pl.semaphore_wait(barrier, len(order_a) + beside)

    noise_line = line_gather(
        volume_ref, place, depth, line_sem.at[0], line_sem.at[1], line_sem.at[2], line_sem.at[3]
    )
    first = doubling(weight_a, order_a, rank, send_sem.at[0], recv_sem.at[0])
    second = doubling(weight_b, order_b, rank, send_sem.at[1], recv_sem.at[1])
    third = doubling(moment_a, order_a, rank, send_sem.at[2], recv_sem.at[2])
    fourth = doubling(moment_b, order_b, rank, send_sem.at[3], recv_sem.at[3])
    share_lines = [
        line_gather(slots, place, depth, *[line_sem.at[4 * k + j] for j in range(4)])
        for k, slots in ((1, kernels_a), (2, kernels_b))
    ]
    advance(first, second, noise_line)

    lane = lax.broadcasted_iota(jnp.int32, (wide, X), 1)
    blocks = [
        [jnp.concatenate([disc_ref[4 * a + 2 * b + d] for b in range(2)], axis=0) for d in range(2)]
        for a in range(2)
    ]
    for a in range(2):
        for d in range(2):
            at = 2 * a + d
            critic_back_ref[a * wide : (a + 1) * wide, d * X : (d + 1) * X] = blocks[a][d]
            critic_ref[:, at * wide : (at + 1) * wide] = (
                blocks[a][d].astype(jnp.float32).T.astype(jnp.bfloat16)
            )
    empty = jnp.zeros((3 * wide, X), jnp.bfloat16)
    for buffer in [inputs_ref.at[k] for k in range(3)] + [grads_ref.at[k] for k in range(2)]:
        buffer[:, 0:X] = empty
        buffer[:, cells + X : cells + 2 * X] = empty

    while advance(first, second):
        advance(noise_line)

    keep = flags_ref[rank] == 1
    partner = pairing_ref[rank]
    picks = []
    for order in (order_a, order_b):
        pick = 0
        for k, bit in enumerate(order):
            differs = lax.rem(rank // bit + partner // bit, 2)
            pick = pick + differs * (1 << k)
        picks.append(jnp.where(keep, 0, pick))
    kernels_a[place] = weight_a[picks[0]]
    kernels_b[place] = weight_b[picks[1]]
    advance(*share_lines, third, fourth)

    def put(buffer, plane, value):
        columns = pl.ds((plane + 1) * X, X)
        low = jnp.where(lane == 0, 0.0, pltpu.roll(value, 1, 1))
        high = jnp.where(lane == X - 1, 0.0, pltpu.roll(value, X - 1, 1))
        buffer[0:wide, columns] = low.astype(jnp.bfloat16)
        buffer[wide : 2 * wide, columns] = value.astype(jnp.bfloat16)
        buffer[2 * wide : 3 * wide, columns] = high.astype(jnp.bfloat16)

    def near_rows(low, high):
        return jnp.concatenate([low, high], axis=0).astype(jnp.float32)[:share_rows]

    def unpack(part):
        rows = near_rows(kernels_a[part], kernels_b[part])
        begin = pl.multiple_of(2 * part * share_rows, 8)
        square_ref[pl.ds(begin, share_rows, stride=2), :] = rows[:, :channels]
        square_ref[pl.ds(begin + 1, share_rows, stride=2), :] = rows[:, channels:]

    def tap(layer, a, b, c):
        begin = (27 * layer + 9 * a + 3 * b + c) * channels
        return square_ref[begin : begin + channels, :]

    def prepare(layer):
        for a in range(3):
            for c in range(3):
                middle = tap(layer, a, 1, c)
                block = jnp.concatenate(
                    [
                        jnp.concatenate([middle, tap(layer, a, 2, c)], axis=1),
                        jnp.concatenate([tap(layer, a, 0, c), middle], axis=1),
                    ],
                    axis=0,
                )
                fore_ref[layer, a, :, c * wide : (c + 1) * wide] = block.astype(jnp.bfloat16)
                if layer:
                    back_ref[layer - 1, 2 - a, :, (2 - c) * wide : (3 - c) * wide] = (
                        block.T.astype(jnp.bfloat16)
                    )

    def convolved(weights, buffer, pair):
        total = None
        for a in range(3):
            columns = pl.ds((2 * pair + a) * X, 2 * X)
            term = dot(weights[a], buffer[:, columns])
            total = term if total is None else total + term
        return total

    def forward(layer):
        prepare(layer)

        for pair in range(planes // 2):
            total = convolved(fore_ref.at[layer], inputs_ref.at[layer], pair)
            if layer < 2:
                pre_ref[layer, :, 2 * pair * X : (2 * pair + 2) * X] = total
                act = gelu_of(total)
                put(inputs_ref.at[layer + 1], 2 * pair, act[:, :X])
                put(inputs_ref.at[layer + 1], 2 * pair + 1, act[:, X:])
            else:
                criticise(pair, jnp.tanh(total))

    score = jnp.broadcast_to(score_ref[...], (X, X)).T

    def criticise(pair, made):
        rounded = made.astype(jnp.bfloat16)
        exact = rounded.astype(jnp.float32)
        for a in range(2):
            plane = rounded[:, a * X : (a + 1) * X]
            made_all[2 * pair + a, :, 0:X] = plane[:channels]
            made_all[2 * pair + a, :, X : 2 * X] = plane[channels:]
        pieces = []
        for a in range(2):
            plane = exact[:, a * X : (a + 1) * X]
            pieces += [plane, pltpu.roll(plane, X - 1, 1)]
        response = dot(critic_ref[...], jnp.concatenate(pieces, axis=0).astype(jnp.bfloat16))
        scores = jnp.sum(score * gelu_of(response), axis=0, keepdims=True)
        slope = -jax.nn.sigmoid(-scores)
        upstream = gelu_slope(response) * (slope * score)
        upstream = jnp.where(lax.rem(lane, 2) == 0, upstream, 0.0)
        pieces = jnp.concatenate([upstream, pltpu.roll(upstream, 1, 1)], axis=0)
        spread = dot(critic_back_ref[...], pieces.astype(jnp.bfloat16))
        for a in range(2):
            plane = made[:, a * X : (a + 1) * X]
            fall = 1.0 - plane * plane
            put(grads_ref.at[0], 2 * pair + a, spread[a * wide : (a + 1) * wide] * fall)

    unpack(place)
    while advance(noise_line):
        pass
    for part in range(depth):

        for plane in range(own):
            both = volume_ref[part, plane].astype(jnp.float32)
            whole = jnp.concatenate([both[:, :X], both[:, X:]], axis=0)
            put(inputs_ref.at[0], part * own + plane, whole)

    layer_rows = 27 * channels
    edges = []
    for layer in range(3):
        edges.append((layer * layer_rows // (2 * share_rows), ((layer + 1) * layer_rows - 1) // (2 * share_rows)))

    def ready(layer, at):
        before = ready(layer - 1, at) if layer else 0
        last = max(abs(edge - at) for edge in edges[layer])
        return max(before, layer + 1 if last <= layer + 1 < depth else depth - 1)

    for step in range(depth):
        if step:
            advance(*share_lines)
            advance(third, fourth)

            @pl.when(place >= step)
            def _():
                unpack(place - step)

            @pl.when(place + step <= depth - 1)
            def _():
                unpack(place + step)

        for layer in range(3):
            places = [at for at in range(depth) if ready(layer, at) == step]
            if places:
                here = place == places[0]
                for at in places[1:]:
                    here = here | (place == at)

                @pl.when(here)
                def _():
                    forward(layer)

    begin = 2 * place * share_rows

    def kernel_sums(layer, gradient):
        for a in range(3):
            low = (27 * layer + 9 * a) * channels

            @pl.when((low + 9 * channels > begin) & (low < begin + 2 * share_rows))
            def _():
                sums = dot_rows(gradient[...], inputs_ref[layer, :, a * X : a * X + cells])
                for c in range(3):
                    block = sums[:, c * wide : (c + 1) * wide]
                    parts = (
                        block[channels:, :channels],
                        block[:channels, :channels] + block[channels:, channels:],
                        block[:channels, channels:],
                    )
                    for b in range(3):
                        row = low + (3 * b + c) * channels
                        square_ref[row : row + channels, :] = parts[b]

    for layer in (2, 1):
        held = grads_ref.at[2 - layer]
        kernel_sums(layer, held.at[wide : 2 * wide, X : X + cells])

        @pl.when(begin < layer * layer_rows)
        def _():
            for pair in range(planes // 2):
                columns = pl.ds(2 * pair * X, 2 * X)
                total = convolved(back_ref.at[layer - 1], held, pair)
                total = total * gelu_slope(pre_ref[layer - 1, :, columns])
                if layer == 2:
                    put(grads_ref.at[1], 2 * pair, total[:, :X])
                    put(grads_ref.at[1], 2 * pair + 1, total[:, X:])
                else:
                    later = pl.ds((2 * pair + 1) * X, 2 * X)
                    grads_ref[0, wide : 2 * wide, later] = total.astype(jnp.bfloat16)

    kernel_sums(0, grads_ref.at[0, wide : 2 * wide, X : X + cells])

    while advance(*share_lines, third, fourth):
        pass
    made_ref[...] = made_all[pl.ds(place * own, own)]
    sums = jnp.concatenate(
        [
            square_ref[pl.ds(begin, share_rows, stride=2), :],
            square_ref[pl.ds(begin + 1, share_rows, stride=2), :],
        ],
        axis=1,
    )

    def adopted(mine, near):
        return jnp.where(keep, mine, near)

    near_moment = near_rows(moment_a[picks[0]], moment_b[picks[1]])
    near_weight = near_rows(kernels_a[place], kernels_b[place])
    moment = momentum_decay * adopted(moment_ref[...], near_moment) + sums
    new_moment_ref[...] = moment
    new_weight_ref[...] = adopted(weight_ref[...], near_weight) - step_length * moment


def on_device(trainers, depth, noise, gen_weight, gen_momentum, disc_weight, score_weight, pairing, flags):
    own, channels = noise.shape[1], noise.shape[2]
    planes = own * depth
    if planes > WHOLE_PLANES or depth < 2 or trainers & (trainers - 1):
        return on_device_split(
            noise, gen_weight, gen_momentum, disc_weight, score_weight, pairing, flags
        )
    weight, moment = gen_weight.reshape(-1, X), gen_momentum.reshape(-1, X)
    rows = weight.shape[0]
    half = -(-rows // 32) * 16
    levels = trainers.bit_length() - 1
    wide = 2 * channels
    framed = (planes + 2) * X
    vmem = pl.BlockSpec(memory_space=pltpu.VMEM)
    smem = pl.BlockSpec(memory_space=pltpu.SMEM)
    slots = pltpu.VMEM((trainers, half, X), jnp.bfloat16)
    made, new_weight, new_moment = pl.pallas_call(
        functools.partial(round_kernel, trainers, depth),
        out_shape=(
            jax.ShapeDtypeStruct(noise.shape[1:], jnp.bfloat16),
            jax.ShapeDtypeStruct(weight.shape, jnp.float32),
            jax.ShapeDtypeStruct(weight.shape, jnp.float32),
        ),
        in_specs=[smem] * 2 + [vmem] * 5,
        out_specs=(vmem,) * 3,
        scratch_shapes=[
            pltpu.VMEM((depth, half, X), jnp.bfloat16),
            pltpu.VMEM((depth, half, X), jnp.bfloat16),
            pltpu.VMEM((depth,) + noise.shape[1:], jnp.bfloat16),
            slots,
            slots,
            slots,
            slots,
            pltpu.VMEM((81 * channels, channels), jnp.float32),
            pltpu.VMEM((3, 3, wide, 3 * wide), jnp.bfloat16),
            pltpu.VMEM((2, 3, wide, 3 * wide), jnp.bfloat16),
            pltpu.VMEM((3, 3 * wide, framed), jnp.bfloat16),
            pltpu.VMEM((2, 3 * wide, framed), jnp.bfloat16),
            pltpu.VMEM((2, wide, planes * X), jnp.float32),
            pltpu.VMEM((planes,) + noise.shape[2:], jnp.bfloat16),
            pltpu.VMEM((X, 4 * wide), jnp.bfloat16),
            pltpu.VMEM((2 * wide, 2 * X), jnp.bfloat16),
            pltpu.SemaphoreType.DMA((4, levels)),
            pltpu.SemaphoreType.DMA((4, levels)),
            pltpu.SemaphoreType.DMA((12, depth - 1)),
        ],
        compiler_params=pltpu.CompilerParams(
            collective_id=0, has_side_effects=True, vmem_limit_bytes=VMEM_LIMIT
        ),
    )(
        pairing,
        flags,
        weight,
        moment,
        noise[0],
        disc_weight[0].swapaxes(1, 2),
        score_weight,
    )
    return made[None], new_weight.reshape(gen_weight.shape), new_moment.reshape(gen_weight.shape)


def solution(mesh):
    placed = (
        P("trainer", "depth", None, None),
        P("trainer", "depth"),
        P("trainer", "depth"),
        P("trainer", None, None, None),
        P("trainer", None),
        P(),
        P(),
    )
    return jax.shard_map(
        functools.partial(on_device, mesh.shape["trainer"], mesh.shape["depth"]),
        mesh=mesh,
        in_specs=placed,
        out_specs=(P("trainer", "depth", None, None), P("trainer", "depth"), P("trainer", "depth")),
        check_vma=False,
    )
```

```python
import functools

import jax
import jax.numpy as jnp
from jax import lax
from jax.experimental import pallas as pl
from jax.experimental.pallas import tpu as pltpu
from jax.sharding import PartitionSpec as P

Y = 2
X = 128


momentum_decay = 0.9
step_length = 0.01


def extended(block, sides, width):
    for axis, dim in sides:
        count = lax.axis_size(axis)
        forward = [(i, i + 1) for i in range(count - 1)]
        backward = [(target, source) for source, target in forward]
        low = lax.ppermute(
            lax.slice_in_dim(block, block.shape[dim] - width, None, axis=dim), axis, forward
        )
        high = lax.ppermute(lax.slice_in_dim(block, 0, width, axis=dim), axis, backward)
        block = jnp.concatenate([low, block, high], axis=dim)
    return block


def framed_copies(padded):
    breadth = X
    cells = padded.shape[2]
    framed = jnp.pad(padded, ((0, 0), (0, 0), (breadth + 1, breadth + 1)))
    column = (jnp.arange(cells + 2 * breadth + 2, dtype=jnp.int32) - breadth - 1) % breadth
    left_copy = jnp.where(
        (column == breadth - 1)[None, None, :], jnp.zeros((), framed.dtype), framed
    )
    right_copy = jnp.where((column == 0)[None, None, :], jnp.zeros((), framed.dtype), framed)
    return (left_copy, framed, right_copy)


def stacked_window(copies, read_y, cells):
    breadth = X
    parts_list = []
    for read_x in range(3):
        begin = read_y * breadth + read_x
        parts_list.append(copies[read_x][:, :, begin : begin + cells])
    return jnp.concatenate(parts_list, axis=1)


def group_kernel(layer):
    channels = layer.shape[-1]
    cube = layer.reshape(3, 3, 3, channels, channels)
    return cube.transpose(0, 1, 3, 2, 4).reshape(3, 3, channels, 3 * channels)


def flip_kernel(layer):
    channels = layer.shape[-1]
    cube = layer.reshape(3, 3, 3, channels, channels)[::-1, ::-1, ::-1].swapaxes(3, 4)
    return cube.transpose(0, 1, 3, 2, 4).reshape(3, 3, channels, 3 * channels)


def convolve_grouped(padded, grouped):
    planes, cells = (padded.shape[0] - 2, padded.shape[2])
    copies = framed_copies(padded)
    summed = jnp.zeros((planes, grouped.shape[2], cells), jnp.float32)
    for read_y in range(3):
        window = stacked_window(copies, read_y, cells)
        for read_z in range(3):
            summed = summed + jnp.einsum(
                "oj,zjs->zos",
                grouped[read_z, read_y],
                window[read_z : read_z + planes],
                preferred_element_type=jnp.float32,
            )
    return summed


def convolve(padded, layer):
    return convolve_grouped(padded, group_kernel(layer))


def convolve_back(padded, layer):
    return convolve_grouped(padded, flip_kernel(layer))


def kernel_grad(gradient, padded):
    planes, channels_out, cells = gradient.shape
    channels_in = padded.shape[1]
    copies = framed_copies(padded)
    rows_list = []
    for read_z in range(3):
        row_list = []
        for read_y in range(3):
            window = stacked_window(copies, read_y, cells)
            row_list.append(
                jnp.einsum(
                    "zos,zjs->oj",
                    gradient,
                    window[read_z : read_z + planes],
                    preferred_element_type=jnp.float32,
                )
            )
        rows_list.append(jnp.stack(row_list))
    grouped = jnp.stack(rows_list)
    return (
        grouped.reshape(3, 3, channels_out, 3, channels_in)
        .transpose(0, 1, 3, 2, 4)
        .reshape(27, channels_out, channels_in)
    )


def gelu_back(inputs, upstream):
    return jax.vjp(jax.nn.gelu, inputs)[1](upstream)[0]


def widen_back(gradient):
    return extended(gradient, (("depth", 0),), 1)


def widen_forward(volume):
    return extended(volume, (("depth", 0),), 1)


def critic_grad(generated, disc_kernel, score_vector):
    planes, channels, cells = generated.shape
    blocks = generated.reshape(planes // 2, 2, channels, Y // 2, 2, X // 2, 2)
    kernel_cube = disc_kernel.reshape(2, 2, 2, disc_kernel.shape[1], channels)
    response = jnp.einsum(
        "abdoc,zacybxd->zoyx", kernel_cube, blocks, preferred_element_type=jnp.float32
    )
    features = jax.nn.gelu(response)
    scores = jnp.sum(score_vector[None, :, None, None] * features, axis=1)
    slope = -jax.nn.sigmoid(-scores)
    upstream = gelu_back(response, slope[:, None] * score_vector[None, :, None, None]).astype(
        jnp.bfloat16
    )
    spread = jnp.einsum(
        "abdoc,zoyx->zacybxd", kernel_cube, upstream, preferred_element_type=jnp.float32
    )
    return spread.reshape(planes, channels, cells)


def on_device_split(noise, gen_weight, gen_momentum, disc_weight, score_weight, pairing, flags):
    trainer_rank = lax.axis_index("trainer")
    partner = pairing[trainer_rank]
    keeper = flags[trainer_rank] == 1
    trainer_count = lax.axis_size("trainer")
    own_pair = jnp.concatenate([gen_weight, gen_momentum], axis=0)
    slot_ids = jnp.arange(trainer_count, dtype=jnp.int32)
    outgoing = jnp.where((slot_ids == partner)[:, None, None], own_pair[None], 0.0)
    incoming = lax.all_to_all(
        outgoing.astype(jnp.bfloat16), "trainer", split_axis=0, concat_axis=0, tiled=True
    ).astype(outgoing.dtype)
    arrived = lax.dynamic_index_in_dim(incoming, partner, 0, keepdims=False)
    other_weight, other_moment = (arrived[0:1], arrived[1:2])
    chosen_weight = jnp.where(keeper, gen_weight, other_weight)
    chosen_momentum = jnp.where(keeper, gen_momentum, other_moment)
    channels = noise.shape[2]
    all_kernels = lax.all_gather(chosen_weight.astype(jnp.bfloat16), "depth", axis=1, tiled=True)
    layers = all_kernels.reshape(3, 27, channels, channels)
    latent = noise[0]
    latent_pad = widen_forward(latent)
    first_pre = convolve(latent_pad, layers[0])
    first_act_pad = widen_forward(jax.nn.gelu(first_pre).astype(jnp.bfloat16))
    second_pre = convolve(first_act_pad, layers[1])
    second_act_pad = widen_forward(jax.nn.gelu(second_pre).astype(jnp.bfloat16))
    third_pre = convolve(second_act_pad, layers[2])
    output_f = jnp.tanh(third_pre)
    generated = output_f.astype(jnp.bfloat16)
    gen_grad = critic_grad(generated, disc_weight[0], score_weight[0])
    third_grad = (gen_grad * (1.0 - output_f * output_f)).astype(jnp.bfloat16)
    grad_three = kernel_grad(third_grad, second_act_pad)
    second_back = convolve_back(widen_back(third_grad), layers[2])
    second_grad = gelu_back(second_pre, second_back).astype(jnp.bfloat16)
    grad_two = kernel_grad(second_grad, first_act_pad)
    first_back = convolve_back(widen_back(second_grad), layers[1])
    first_grad = gelu_back(first_pre, first_back).astype(jnp.bfloat16)
    grad_one = kernel_grad(first_grad, latent_pad)
    local_grad = jnp.concatenate(
        [grad_one.reshape(-1), grad_two.reshape(-1), grad_three.reshape(-1)]
    )
    share_len = gen_weight.shape[1]
    grad_whole = lax.psum(local_grad.astype(jnp.bfloat16), "depth").astype(jnp.float32)
    grad_share = lax.dynamic_slice_in_dim(
        grad_whole, lax.axis_index("depth") * share_len, share_len, 0
    )
    new_momentum = momentum_decay * chosen_momentum + grad_share[None, :]
    new_weight = chosen_weight - step_length * new_momentum
    return (generated[None], new_weight, new_momentum)


MESH = pl.DeviceIdType.MESH
VMEM_LIMIT = 56 * 1024 * 1024
WHOLE_PLANES = 16
PIECES = 4


def bit_orders(count):
    bits = [1 << k for k in range(count.bit_length() - 1)]
    return bits[1:] + bits[:1], bits[:0:-1] + bits[:1]


def flipped(index, bit):
    return index + bit - 2 * bit * lax.rem(index // bit, 2)


def doubling(slots, order, rank, send_sem, recv_sem):
    for k, bit in enumerate(order):
        copy = pltpu.make_async_remote_copy(
            src_ref=slots.at[pl.ds(0, 1 << k)],
            dst_ref=slots.at[pl.ds(1 << k, 1 << k)],
            send_sem=send_sem.at[k],
            recv_sem=recv_sem.at[k],
            device_id={"trainer": flipped(rank, bit)},
            device_id_type=MESH,
        )
        copy.start()
        yield
        copy.wait()


def line_gather(slots, place, count, up_send, up_recv, down_send, down_recv):
    def move(slot, target, send_sem, recv_sem):
        return pltpu.make_async_remote_copy(
            src_ref=slots.at[slot],
            dst_ref=slots.at[slot],
            send_sem=send_sem,
            recv_sem=recv_sem,
            device_id={"depth": target},
            device_id_type=MESH,
        )

    def up(step):
        return move(jnp.maximum(place - step, 0), place + 1, up_send.at[step], up_recv.at[step])

    def down(step):
        return move(
            jnp.minimum(place + step, count - 1), place - 1, down_send.at[step], down_recv.at[step]
        )

    for step in range(count - 1):

        @pl.when((place < count - 1) & (place >= step))
        def _():
            up(step).start()

        @pl.when((place > 0) & (place + step <= count - 1))
        def _():
            down(step).start()

        yield

        @pl.when(place >= step + 1)
        def _():
            up(step).wait_recv()

        @pl.when(place + step + 1 <= count - 1)
        def _():
            down(step).wait_recv()

    yield
    for step in range(count - 1):

        @pl.when((place < count - 1) & (place >= step))
        def _():
            up(step).wait_send()

        @pl.when((place > 0) & (place + step <= count - 1))
        def _():
            down(step).wait_send()


def advance(*steps):
    alive = False
    for each in steps:
        alive = next(each, 0) is None or alive
    return alive


ROOT = 0.7978845608028654
CUBIC = 0.044715


def gelu_of(inputs):
    bend = jnp.tanh(ROOT * (inputs + CUBIC * (inputs * inputs * inputs)))
    return 0.5 * inputs * (1.0 + bend)


def gelu_slope(inputs):
    square = inputs * inputs
    bend = jnp.tanh(ROOT * (inputs + CUBIC * (square * inputs)))
    tilt = ROOT * (1.0 + 3.0 * CUBIC * square)
    return 0.5 * (1.0 + bend) + 0.5 * inputs * (1.0 - bend * bend) * tilt


def dot(left, right):
    return jnp.dot(left, right, preferred_element_type=jnp.float32)


def dot_rows(left, right):
    return lax.dot_general(
        left, right, (((1,), (1,)), ((), ())), preferred_element_type=jnp.float32
    )


def round_kernel(
    trainers,
    depth,
    pairing_ref,
    flags_ref,
    weight_hbm,
    moment_hbm,
    noise_hbm,
    disc_hbm,
    score_ref,
    made_ref,
    new_weight_ref,
    new_moment_ref,
    weight_ref,
    moment_ref,
    disc_ref,
    volume_ref,
    moment_a,
    moment_b,
    square_ref,
    fore_ref,
    back_ref,
    inputs_ref,
    grads_ref,
    pre_ref,
    made_all,
    critic_ref,
    critic_back_ref,
    load_sem,
    send_sem,
    recv_sem,
    line_sem,
    *piece_refs,
):
    slots, kernels = piece_refs[:PIECES], piece_refs[PIECES:]
    own, channels = noise_hbm.shape[0], noise_hbm.shape[1]
    planes = own * depth
    wide = 2 * channels
    cells = planes * X
    share_rows = weight_ref.shape[0]
    rank = lax.axis_index("trainer")
    place = lax.axis_index("depth")
    order_a, order_b = bit_orders(trainers)
    orders = (order_a, order_b) * (PIECES // 2)
    loads = [
        pltpu.make_async_copy(source, target, load_sem.at[k])
        for k, (source, target) in enumerate(
            (
                (weight_hbm, weight_ref),
                (noise_hbm, volume_ref.at[place]),
                (disc_hbm, disc_ref),
                (moment_hbm, moment_ref),
            )
        )
    ]
    for load in loads:
        load.start()
    barrier = pltpu.get_barrier_semaphore()
    for bit in order_a:
        pl.semaphore_signal(
            barrier, inc=1, device_id={"trainer": flipped(rank, bit)}, device_id_type=MESH
        )

    @pl.when(place > 0)
    def _():
        pl.semaphore_signal(barrier, inc=1, device_id={"depth": place - 1}, device_id_type=MESH)

    @pl.when(place < depth - 1)
    def _():
        pl.semaphore_signal(barrier, inc=1, device_id={"depth": place + 1}, device_id_type=MESH)

    def cut(source, begin, rows):
        piece = source[begin : min(begin + rows, share_rows)]
        lack = rows - piece.shape[0]
        if lack:
            padding = jnp.zeros((lack, piece.shape[1]), jnp.float32)
            piece = jnp.concatenate([piece, padding], axis=0)
        return piece.astype(jnp.bfloat16)

    loads[0].wait()
    begin = 0
    for piece in slots:
        piece[0] = cut(weight_ref, begin, piece.shape[1])
        begin += piece.shape[1]
    loads[1].wait()

    beside = (place > 0).astype(jnp.int32) + (place < depth - 1).astype(jnp.int32)
    pl.semaphore_wait(barrier, len(order_a) + beside)

    noise_line = line_gather(
        volume_ref, place, depth, line_sem.at[0], line_sem.at[1], line_sem.at[2], line_sem.at[3]
    )
    near = [
        doubling(piece, order, rank, send_sem.at[k], recv_sem.at[k])
        for k, (piece, order) in enumerate(zip(slots, orders))
    ]
    third = doubling(moment_a, order_a, rank, send_sem.at[PIECES], recv_sem.at[PIECES])
    fourth = doubling(moment_b, order_b, rank, send_sem.at[PIECES + 1], recv_sem.at[PIECES + 1])
    share_lines = [
        line_gather(piece, place, depth, *[line_sem.at[4 * k + 4 + j] for j in range(4)])
        for k, piece in enumerate(kernels)
    ]
    groups = [slice(k, k + 2) for k in range(0, PIECES, 2)]
    advance(*near[groups[0]], noise_line)
    loads[2].wait()

    lane = lax.broadcasted_iota(jnp.int32, (wide, X), 1)
    blocks = [
        [jnp.concatenate([disc_ref[4 * a + 2 * b + d] for b in range(2)], axis=0) for d in range(2)]
        for a in range(2)
    ]
    for a in range(2):
        for d in range(2):
            at = 2 * a + d
            critic_back_ref[a * wide : (a + 1) * wide, d * X : (d + 1) * X] = blocks[a][d]
            critic_ref[:, at * wide : (at + 1) * wide] = (
                blocks[a][d].astype(jnp.float32).T.astype(jnp.bfloat16)
            )
    empty = jnp.zeros((3 * wide, X), jnp.bfloat16)
    for buffer in [inputs_ref.at[k] for k in range(3)] + [grads_ref.at[k] for k in range(2)]:
        buffer[:, 0:X] = empty
        buffer[:, cells + X : cells + 2 * X] = empty

    keep = flags_ref[rank] == 1
    partner = pairing_ref[rank]
    picks = []
    for order in (order_a, order_b):
        pick = 0
        for k, bit in enumerate(order):
            differs = lax.rem(rank // bit + partner // bit, 2)
            pick = pick + differs * (1 << k)
        picks.append(jnp.where(keep, 0, pick))
    levels = len(order_a)
    for tick in range(1, levels + len(groups)):
        for k, group in enumerate(groups):
            if 0 <= tick - k <= levels:
                advance(*near[group])
            if tick - k == levels:
                for at in range(PIECES)[group]:
                    kernels[at][place] = slots[at][picks[at % 2]]
                advance(*share_lines[group])
        if tick < levels + 1:
            advance(noise_line)
    loads[3].wait()
    half = moment_a.shape[1]
    moment_a[0] = cut(moment_ref, 0, half)
    moment_b[0] = cut(moment_ref, half, half)
    advance(third, fourth)

    def put(buffer, plane, value):
        columns = pl.ds((plane + 1) * X, X)
        low = jnp.where(lane == 0, 0.0, pltpu.roll(value, 1, 1))
        high = jnp.where(lane == X - 1, 0.0, pltpu.roll(value, X - 1, 1))
        buffer[0:wide, columns] = low.astype(jnp.bfloat16)
        buffer[wide : 2 * wide, columns] = value.astype(jnp.bfloat16)
        buffer[2 * wide : 3 * wide, columns] = high.astype(jnp.bfloat16)

    def near_rows(*rows):
        return jnp.concatenate(rows, axis=0).astype(jnp.float32)[:share_rows]

    def unpack(part):
        rows = near_rows(*[piece[part] for piece in kernels])
        begin = pl.multiple_of(2 * part * share_rows, 8)
        square_ref[pl.ds(begin, share_rows, stride=2), :] = rows[:, :channels]
        square_ref[pl.ds(begin + 1, share_rows, stride=2), :] = rows[:, channels:]

    def tap(layer, a, b, c):
        begin = (27 * layer + 9 * a + 3 * b + c) * channels
        return square_ref[begin : begin + channels, :]

    def prepare(layer):
        for a in range(3):
            for c in range(3):
                middle = tap(layer, a, 1, c)
                block = jnp.concatenate(
                    [
                        jnp.concatenate([middle, tap(layer, a, 2, c)], axis=1),
                        jnp.concatenate([tap(layer, a, 0, c), middle], axis=1),
                    ],
                    axis=0,
                )
                fore_ref[layer, a, :, c * wide : (c + 1) * wide] = block.astype(jnp.bfloat16)
                if layer:
                    back_ref[layer - 1, 2 - a, :, (2 - c) * wide : (3 - c) * wide] = (
                        block.T.astype(jnp.bfloat16)
                    )

    def convolved(weights, buffer, pair):
        total = None
        for a in range(3):
            columns = pl.ds((2 * pair + a) * X, 2 * X)
            term = dot(weights[a], buffer[:, columns])
            total = term if total is None else total + term
        return total

    def forward(layer):
        for pair in range(planes // 2):
            total = convolved(fore_ref.at[layer], inputs_ref.at[layer], pair)
            if layer < 2:
                pre_ref[layer, :, 2 * pair * X : (2 * pair + 2) * X] = total
                act = gelu_of(total)
                put(inputs_ref.at[layer + 1], 2 * pair, act[:, :X])
                put(inputs_ref.at[layer + 1], 2 * pair + 1, act[:, X:])
            else:
                criticise(pair, jnp.tanh(total))

    score = jnp.broadcast_to(score_ref[...], (X, X)).T

    def criticise(pair, made):
        rounded = made.astype(jnp.bfloat16)
        exact = rounded.astype(jnp.float32)
        for a in range(2):
            plane = rounded[:, a * X : (a + 1) * X]
            made_all[2 * pair + a, :, 0:X] = plane[:channels]
            made_all[2 * pair + a, :, X : 2 * X] = plane[channels:]
        pieces = []
        for a in range(2):
            plane = exact[:, a * X : (a + 1) * X]
            pieces += [plane, pltpu.roll(plane, X - 1, 1)]
        response = dot(critic_ref[...], jnp.concatenate(pieces, axis=0).astype(jnp.bfloat16))
        scores = jnp.sum(score * gelu_of(response), axis=0, keepdims=True)
        slope = -jax.nn.sigmoid(-scores)
        upstream = gelu_slope(response) * (slope * score)
        upstream = jnp.where(lax.rem(lane, 2) == 0, upstream, 0.0)
        pieces = jnp.concatenate([upstream, pltpu.roll(upstream, 1, 1)], axis=0)
        spread = dot(critic_back_ref[...], pieces.astype(jnp.bfloat16))
        for a in range(2):
            plane = made[:, a * X : (a + 1) * X]
            fall = 1.0 - plane * plane
            put(grads_ref.at[0], 2 * pair + a, spread[a * wide : (a + 1) * wide] * fall)

    unpack(place)
    while advance(noise_line):
        pass
    for part in range(depth):

        for plane in range(own):
            both = volume_ref[part, plane].astype(jnp.float32)
            whole = jnp.concatenate([both[:, :X], both[:, X:]], axis=0)
            put(inputs_ref.at[0], part * own + plane, whole)

    layer_rows = 27 * channels
    edges = []
    for layer in range(3):
        edges.append((layer * layer_rows // (2 * share_rows), ((layer + 1) * layer_rows - 1) // (2 * share_rows)))

    def known(layer, at):
        return max(abs(edge - at) for edge in edges[layer])

    def ready(layer, at):
        before = ready(layer - 1, at) if layer else 0
        last = known(layer, at)
        return max(before, layer + 1 if last <= layer + 1 < depth else depth - 1)

    for step in range(depth):
        if step:
            advance(*share_lines)
            advance(third, fourth)

            @pl.when(place >= step)
            def _():
                unpack(place - step)

            @pl.when(place + step <= depth - 1)
            def _():
                unpack(place + step)

        for act, due in ((prepare, known), (forward, ready)):
            for layer in range(3):
                places = [at for at in range(depth) if due(layer, at) == step]
                if places:
                    here = place == places[0]
                    for at in places[1:]:
                        here = here | (place == at)

                    @pl.when(here)
                    def _():
                        act(layer)

    begin = 2 * place * share_rows

    def kernel_sums(layer, gradient):
        for a in range(3):
            low = (27 * layer + 9 * a) * channels

            @pl.when((low + 9 * channels > begin) & (low < begin + 2 * share_rows))
            def _():
                sums = dot_rows(gradient[...], inputs_ref[layer, :, a * X : a * X + cells])
                for c in range(3):
                    block = sums[:, c * wide : (c + 1) * wide]
                    parts = (
                        block[channels:, :channels],
                        block[:channels, :channels] + block[channels:, channels:],
                        block[:channels, channels:],
                    )
                    for b in range(3):
                        row = low + (3 * b + c) * channels
                        square_ref[row : row + channels, :] = parts[b]

    for layer in (2, 1):
        held = grads_ref.at[2 - layer]
        kernel_sums(layer, held.at[wide : 2 * wide, X : X + cells])

        @pl.when(begin < layer * layer_rows)
        def _():
            for pair in range(planes // 2):
                columns = pl.ds(2 * pair * X, 2 * X)
                total = convolved(back_ref.at[layer - 1], held, pair)
                total = total * gelu_slope(pre_ref[layer - 1, :, columns])
                if layer == 2:
                    put(grads_ref.at[1], 2 * pair, total[:, :X])
                    put(grads_ref.at[1], 2 * pair + 1, total[:, X:])
                else:
                    later = pl.ds((2 * pair + 1) * X, 2 * X)
                    grads_ref[0, wide : 2 * wide, later] = total.astype(jnp.bfloat16)

    kernel_sums(0, grads_ref.at[0, wide : 2 * wide, X : X + cells])

    while advance(*share_lines, third, fourth):
        pass
    made_ref[...] = made_all[pl.ds(place * own, own)]
    sums = jnp.concatenate(
        [
            square_ref[pl.ds(begin, share_rows, stride=2), :],
            square_ref[pl.ds(begin + 1, share_rows, stride=2), :],
        ],
        axis=1,
    )

    def adopted(mine, near):
        return jnp.where(keep, mine, near)

    near_moment = near_rows(moment_a[picks[0]], moment_b[picks[1]])
    near_weight = near_rows(*[piece[place] for piece in kernels])
    moment = momentum_decay * adopted(moment_ref[...], near_moment) + sums
    new_moment_ref[...] = moment
    new_weight_ref[...] = adopted(weight_ref[...], near_weight) - step_length * moment


def on_device(trainers, depth, noise, gen_weight, gen_momentum, disc_weight, score_weight, pairing, flags):
    own, channels = noise.shape[1], noise.shape[2]
    planes = own * depth
    if planes > WHOLE_PLANES or depth < 2 or trainers & (trainers - 1):
        return on_device_split(
            noise, gen_weight, gen_momentum, disc_weight, score_weight, pairing, flags
        )
    weight, moment = gen_weight.reshape(-1, X), gen_momentum.reshape(-1, X)
    rows = weight.shape[0]
    half = -(-rows // 32) * 16
    units = -(-rows // 16)
    sizes = [16 * ((units + PIECES - 1 - k) // PIECES) for k in range(PIECES)]
    levels = trainers.bit_length() - 1
    wide = 2 * channels
    framed = (planes + 2) * X
    vmem = pl.BlockSpec(memory_space=pltpu.VMEM)
    smem = pl.BlockSpec(memory_space=pltpu.SMEM)
    hbm = pl.BlockSpec(memory_space=pltpu.HBM)
    moments = pltpu.VMEM((trainers, half, X), jnp.bfloat16)
    made, new_weight, new_moment = pl.pallas_call(
        functools.partial(round_kernel, trainers, depth),
        out_shape=(
            jax.ShapeDtypeStruct(noise.shape[1:], jnp.bfloat16),
            jax.ShapeDtypeStruct(weight.shape, jnp.float32),
            jax.ShapeDtypeStruct(weight.shape, jnp.float32),
        ),
        in_specs=[smem] * 2 + [hbm] * 4 + [vmem],
        out_specs=(vmem,) * 3,
        scratch_shapes=[
            pltpu.VMEM(weight.shape, jnp.float32),
            pltpu.VMEM(weight.shape, jnp.float32),
            pltpu.VMEM((8, channels, X), jnp.bfloat16),
            pltpu.VMEM((depth,) + noise.shape[1:], jnp.bfloat16),
            moments,
            moments,
            pltpu.VMEM((81 * channels, channels), jnp.float32),
            pltpu.VMEM((3, 3, wide, 3 * wide), jnp.bfloat16),
            pltpu.VMEM((2, 3, wide, 3 * wide), jnp.bfloat16),
            pltpu.VMEM((3, 3 * wide, framed), jnp.bfloat16),
            pltpu.VMEM((2, 3 * wide, framed), jnp.bfloat16),
            pltpu.VMEM((2, wide, planes * X), jnp.float32),
            pltpu.VMEM((planes,) + noise.shape[2:], jnp.bfloat16),
            pltpu.VMEM((X, 4 * wide), jnp.bfloat16),
            pltpu.VMEM((2 * wide, 2 * X), jnp.bfloat16),
            pltpu.SemaphoreType.DMA((4,)),
            pltpu.SemaphoreType.DMA((PIECES + 2, levels)),
            pltpu.SemaphoreType.DMA((PIECES + 2, levels)),
            pltpu.SemaphoreType.DMA((4 * PIECES + 4, depth - 1)),
        ]
        + [pltpu.VMEM((trainers, size, X), jnp.bfloat16) for size in sizes]
        + [pltpu.VMEM((depth, size, X), jnp.bfloat16) for size in sizes],
        compiler_params=pltpu.CompilerParams(
            collective_id=0, has_side_effects=True, vmem_limit_bytes=VMEM_LIMIT
        ),
    )(
        pairing,
        flags,
        weight,
        moment,
        noise[0],
        disc_weight[0].swapaxes(1, 2),
        score_weight,
    )
    return made[None], new_weight.reshape(gen_weight.shape), new_moment.reshape(gen_weight.shape)


def solution(mesh):
    placed = (
        P("trainer", "depth", None, None),
        P("trainer", "depth"),
        P("trainer", "depth"),
        P("trainer", None, None, None),
        P("trainer", None),
        P(),
        P(),
    )
    return jax.shard_map(
        functools.partial(on_device, mesh.shape["trainer"], mesh.shape["depth"]),
        mesh=mesh,
        in_specs=placed,
        out_specs=(P("trainer", "depth", None, None), P("trainer", "depth"), P("trainer", "depth")),
        check_vma=False,
    )
```

```python
import functools

import jax
import jax.numpy as jnp
from jax import lax
from jax.experimental import pallas as pl
from jax.experimental.pallas import tpu as pltpu
from jax.sharding import PartitionSpec as P

Y = 2
X = 128


momentum_decay = 0.9
step_length = 0.01


def extended(block, sides, width):
    for axis, dim in sides:
        count = lax.axis_size(axis)
        forward = [(i, i + 1) for i in range(count - 1)]
        backward = [(target, source) for source, target in forward]
        low = lax.ppermute(
            lax.slice_in_dim(block, block.shape[dim] - width, None, axis=dim), axis, forward
        )
        high = lax.ppermute(lax.slice_in_dim(block, 0, width, axis=dim), axis, backward)
        block = jnp.concatenate([low, block, high], axis=dim)
    return block


def framed_copies(padded):
    breadth = X
    cells = padded.shape[2]
    framed = jnp.pad(padded, ((0, 0), (0, 0), (breadth + 1, breadth + 1)))
    column = (jnp.arange(cells + 2 * breadth + 2, dtype=jnp.int32) - breadth - 1) % breadth
    left_copy = jnp.where(
        (column == breadth - 1)[None, None, :], jnp.zeros((), framed.dtype), framed
    )
    right_copy = jnp.where((column == 0)[None, None, :], jnp.zeros((), framed.dtype), framed)
    return (left_copy, framed, right_copy)


def stacked_window(copies, read_y, cells):
    breadth = X
    parts_list = []
    for read_x in range(3):
        begin = read_y * breadth + read_x
        parts_list.append(copies[read_x][:, :, begin : begin + cells])
    return jnp.concatenate(parts_list, axis=1)


def group_kernel(layer):
    channels = layer.shape[-1]
    cube = layer.reshape(3, 3, 3, channels, channels)
    return cube.transpose(0, 1, 3, 2, 4).reshape(3, 3, channels, 3 * channels)


def flip_kernel(layer):
    channels = layer.shape[-1]
    cube = layer.reshape(3, 3, 3, channels, channels)[::-1, ::-1, ::-1].swapaxes(3, 4)
    return cube.transpose(0, 1, 3, 2, 4).reshape(3, 3, channels, 3 * channels)


def convolve_grouped(padded, grouped):
    planes, cells = (padded.shape[0] - 2, padded.shape[2])
    copies = framed_copies(padded)
    summed = jnp.zeros((planes, grouped.shape[2], cells), jnp.float32)
    for read_y in range(3):
        window = stacked_window(copies, read_y, cells)
        for read_z in range(3):
            summed = summed + jnp.einsum(
                "oj,zjs->zos",
                grouped[read_z, read_y],
                window[read_z : read_z + planes],
                preferred_element_type=jnp.float32,
            )
    return summed


def convolve(padded, layer):
    return convolve_grouped(padded, group_kernel(layer))


def convolve_back(padded, layer):
    return convolve_grouped(padded, flip_kernel(layer))


def kernel_grad(gradient, padded):
    planes, channels_out, cells = gradient.shape
    channels_in = padded.shape[1]
    copies = framed_copies(padded)
    rows_list = []
    for read_z in range(3):
        row_list = []
        for read_y in range(3):
            window = stacked_window(copies, read_y, cells)
            row_list.append(
                jnp.einsum(
                    "zos,zjs->oj",
                    gradient,
                    window[read_z : read_z + planes],
                    preferred_element_type=jnp.float32,
                )
            )
        rows_list.append(jnp.stack(row_list))
    grouped = jnp.stack(rows_list)
    return (
        grouped.reshape(3, 3, channels_out, 3, channels_in)
        .transpose(0, 1, 3, 2, 4)
        .reshape(27, channels_out, channels_in)
    )


def gelu_back(inputs, upstream):
    return jax.vjp(jax.nn.gelu, inputs)[1](upstream)[0]


def widen_back(gradient):
    return extended(gradient, (("depth", 0),), 1)


def widen_forward(volume):
    return extended(volume, (("depth", 0),), 1)


def critic_grad(generated, disc_kernel, score_vector):
    planes, channels, cells = generated.shape
    blocks = generated.reshape(planes // 2, 2, channels, Y // 2, 2, X // 2, 2)
    kernel_cube = disc_kernel.reshape(2, 2, 2, disc_kernel.shape[1], channels)
    response = jnp.einsum(
        "abdoc,zacybxd->zoyx", kernel_cube, blocks, preferred_element_type=jnp.float32
    )
    features = jax.nn.gelu(response)
    scores = jnp.sum(score_vector[None, :, None, None] * features, axis=1)
    slope = -jax.nn.sigmoid(-scores)
    upstream = gelu_back(response, slope[:, None] * score_vector[None, :, None, None]).astype(
        jnp.bfloat16
    )
    spread = jnp.einsum(
        "abdoc,zoyx->zacybxd", kernel_cube, upstream, preferred_element_type=jnp.float32
    )
    return spread.reshape(planes, channels, cells)


def on_device_split(noise, gen_weight, gen_momentum, disc_weight, score_weight, pairing, flags):
    trainer_rank = lax.axis_index("trainer")
    partner = pairing[trainer_rank]
    keeper = flags[trainer_rank] == 1
    trainer_count = lax.axis_size("trainer")
    own_pair = jnp.concatenate([gen_weight, gen_momentum], axis=0)
    slot_ids = jnp.arange(trainer_count, dtype=jnp.int32)
    outgoing = jnp.where((slot_ids == partner)[:, None, None], own_pair[None], 0.0)
    incoming = lax.all_to_all(
        outgoing.astype(jnp.bfloat16), "trainer", split_axis=0, concat_axis=0, tiled=True
    ).astype(outgoing.dtype)
    arrived = lax.dynamic_index_in_dim(incoming, partner, 0, keepdims=False)
    other_weight, other_moment = (arrived[0:1], arrived[1:2])
    chosen_weight = jnp.where(keeper, gen_weight, other_weight)
    chosen_momentum = jnp.where(keeper, gen_momentum, other_moment)
    channels = noise.shape[2]
    all_kernels = lax.all_gather(chosen_weight.astype(jnp.bfloat16), "depth", axis=1, tiled=True)
    layers = all_kernels.reshape(3, 27, channels, channels)
    latent = noise[0]
    latent_pad = widen_forward(latent)
    first_pre = convolve(latent_pad, layers[0])
    first_act_pad = widen_forward(jax.nn.gelu(first_pre).astype(jnp.bfloat16))
    second_pre = convolve(first_act_pad, layers[1])
    second_act_pad = widen_forward(jax.nn.gelu(second_pre).astype(jnp.bfloat16))
    third_pre = convolve(second_act_pad, layers[2])
    output_f = jnp.tanh(third_pre)
    generated = output_f.astype(jnp.bfloat16)
    gen_grad = critic_grad(generated, disc_weight[0], score_weight[0])
    third_grad = (gen_grad * (1.0 - output_f * output_f)).astype(jnp.bfloat16)
    grad_three = kernel_grad(third_grad, second_act_pad)
    second_back = convolve_back(widen_back(third_grad), layers[2])
    second_grad = gelu_back(second_pre, second_back).astype(jnp.bfloat16)
    grad_two = kernel_grad(second_grad, first_act_pad)
    first_back = convolve_back(widen_back(second_grad), layers[1])
    first_grad = gelu_back(first_pre, first_back).astype(jnp.bfloat16)
    grad_one = kernel_grad(first_grad, latent_pad)
    local_grad = jnp.concatenate(
        [grad_one.reshape(-1), grad_two.reshape(-1), grad_three.reshape(-1)]
    )
    share_len = gen_weight.shape[1]
    grad_whole = lax.psum(local_grad.astype(jnp.bfloat16), "depth").astype(jnp.float32)
    grad_share = lax.dynamic_slice_in_dim(
        grad_whole, lax.axis_index("depth") * share_len, share_len, 0
    )
    new_momentum = momentum_decay * chosen_momentum + grad_share[None, :]
    new_weight = chosen_weight - step_length * new_momentum
    return (generated[None], new_weight, new_momentum)


MESH = pl.DeviceIdType.MESH
VMEM_LIMIT = 56 * 1024 * 1024
WHOLE_PLANES = 16
PIECES = 4


def bit_orders(count):
    bits = [1 << k for k in range(count.bit_length() - 1)]
    return bits[1:] + bits[:1], bits[:0:-1] + bits[:1]


def flipped(index, bit):
    return index + bit - 2 * bit * lax.rem(index // bit, 2)


def doubling(slots, order, rank, send_sem, recv_sem):
    for k, bit in enumerate(order):
        copy = pltpu.make_async_remote_copy(
            src_ref=slots.at[pl.ds(0, 1 << k)],
            dst_ref=slots.at[pl.ds(1 << k, 1 << k)],
            send_sem=send_sem.at[k],
            recv_sem=recv_sem.at[k],
            device_id={"trainer": flipped(rank, bit)},
            device_id_type=MESH,
        )
        copy.start()
        yield
        copy.wait()


def line_gather(slots, place, count, up_send, up_recv, down_send, down_recv):
    def move(slot, target, send_sem, recv_sem):
        return pltpu.make_async_remote_copy(
            src_ref=slots.at[slot],
            dst_ref=slots.at[slot],
            send_sem=send_sem,
            recv_sem=recv_sem,
            device_id={"depth": target},
            device_id_type=MESH,
        )

    def up(step):
        return move(jnp.maximum(place - step, 0), place + 1, up_send.at[step], up_recv.at[step])

    def down(step):
        return move(
            jnp.minimum(place + step, count - 1), place - 1, down_send.at[step], down_recv.at[step]
        )

    for step in range(count - 1):

        @pl.when((place < count - 1) & (place >= step))
        def _():
            up(step).start()

        @pl.when((place > 0) & (place + step <= count - 1))
        def _():
            down(step).start()

        yield

        @pl.when(place >= step + 1)
        def _():
            up(step).wait_recv()

        @pl.when(place + step + 1 <= count - 1)
        def _():
            down(step).wait_recv()

    yield
    for step in range(count - 1):

        @pl.when((place < count - 1) & (place >= step))
        def _():
            up(step).wait_send()

        @pl.when((place > 0) & (place + step <= count - 1))
        def _():
            down(step).wait_send()


def advance(*steps):
    alive = False
    for each in steps:
        alive = next(each, 0) is None or alive
    return alive


ROOT = 0.7978845608028654
CUBIC = 0.044715


def gelu_of(inputs):
    bend = jnp.tanh(ROOT * (inputs + CUBIC * (inputs * inputs * inputs)))
    return 0.5 * inputs * (1.0 + bend)


def gelu_slope(inputs):
    square = inputs * inputs
    bend = jnp.tanh(ROOT * (inputs + CUBIC * (square * inputs)))
    tilt = ROOT * (1.0 + 3.0 * CUBIC * square)
    return 0.5 * (1.0 + bend) + 0.5 * inputs * (1.0 - bend * bend) * tilt


def dot(left, right):
    return jnp.dot(left, right, preferred_element_type=jnp.float32)


def dot_rows(left, right):
    return lax.dot_general(
        left, right, (((1,), (1,)), ((), ())), preferred_element_type=jnp.float32
    )


def round_kernel(
    trainers,
    depth,
    pairing_ref,
    flags_ref,
    weight_hbm,
    moment_hbm,
    noise_hbm,
    disc_hbm,
    score_ref,
    made_ref,
    new_weight_ref,
    new_moment_ref,
    weight_ref,
    moment_ref,
    disc_ref,
    volume_ref,
    moment_a,
    moment_b,
    square_ref,
    fore_ref,
    back_ref,
    inputs_ref,
    grads_ref,
    pre_ref,
    made_all,
    critic_ref,
    critic_back_ref,
    load_sem,
    send_sem,
    recv_sem,
    line_sem,
    *piece_refs,
):
    slots, kernels = piece_refs[:PIECES], piece_refs[PIECES:]
    own, channels = noise_hbm.shape[0], noise_hbm.shape[1]
    planes = own * depth
    wide = 2 * channels
    cells = planes * X
    share_rows = weight_ref.shape[0]
    rank = lax.axis_index("trainer")
    place = lax.axis_index("depth")
    order_a, order_b = bit_orders(trainers)
    orders = (order_a, order_b) * (PIECES // 2)
    loads = [
        pltpu.make_async_copy(source, target, load_sem.at[k])
        for k, (source, target) in enumerate(
            (
                (weight_hbm, weight_ref),
                (noise_hbm, volume_ref.at[place]),
                (disc_hbm, disc_ref),
                (moment_hbm, moment_ref),
            )
        )
    ]
    for load in loads:
        load.start()
    barrier = pltpu.get_barrier_semaphore()
    for bit in order_a:
        pl.semaphore_signal(
            barrier, inc=1, device_id={"trainer": flipped(rank, bit)}, device_id_type=MESH
        )

    @pl.when(place > 0)
    def _():
        pl.semaphore_signal(barrier, inc=1, device_id={"depth": place - 1}, device_id_type=MESH)

    @pl.when(place < depth - 1)
    def _():
        pl.semaphore_signal(barrier, inc=1, device_id={"depth": place + 1}, device_id_type=MESH)

    def cut(source, begin, rows):
        piece = source[begin : min(begin + rows, share_rows)]
        lack = rows - piece.shape[0]
        if lack:
            padding = jnp.zeros((lack, piece.shape[1]), jnp.float32)
            piece = jnp.concatenate([piece, padding], axis=0)
        return piece.astype(jnp.bfloat16)

    loads[0].wait()
    begin = 0
    for piece in slots:
        piece[0] = cut(weight_ref, begin, piece.shape[1])
        begin += piece.shape[1]
    loads[1].wait()

    beside = (place > 0).astype(jnp.int32) + (place < depth - 1).astype(jnp.int32)
    pl.semaphore_wait(barrier, len(order_a) + beside)

    noise_line = line_gather(
        volume_ref, place, depth, line_sem.at[0], line_sem.at[1], line_sem.at[2], line_sem.at[3]
    )
    near = [
        doubling(piece, order, rank, send_sem.at[k], recv_sem.at[k])
        for k, (piece, order) in enumerate(zip(slots, orders))
    ]
    third = doubling(moment_a, order_a, rank, send_sem.at[PIECES], recv_sem.at[PIECES])
    fourth = doubling(moment_b, order_b, rank, send_sem.at[PIECES + 1], recv_sem.at[PIECES + 1])
    share_lines = [
        line_gather(piece, place, depth, *[line_sem.at[4 * k + 4 + j] for j in range(4)])
        for k, piece in enumerate(kernels)
    ]
    groups = [slice(k, k + 2) for k in range(0, PIECES, 2)]
    advance(*near[groups[0]], noise_line)
    loads[2].wait()

    lane = lax.broadcasted_iota(jnp.int32, (wide, X), 1)
    blocks = [
        [jnp.concatenate([disc_ref[4 * a + 2 * b + d] for b in range(2)], axis=0) for d in range(2)]
        for a in range(2)
    ]
    for a in range(2):
        for d in range(2):
            at = 2 * a + d
            critic_back_ref[a * wide : (a + 1) * wide, d * X : (d + 1) * X] = blocks[a][d]
            critic_ref[:, at * wide : (at + 1) * wide] = (
                blocks[a][d].astype(jnp.float32).T.astype(jnp.bfloat16)
            )
    empty = jnp.zeros((3 * wide, X), jnp.bfloat16)
    for buffer in [inputs_ref.at[k] for k in range(3)] + [grads_ref.at[k] for k in range(2)]:
        buffer[:, 0:X] = empty
        buffer[:, cells + X : cells + 2 * X] = empty

    keep = flags_ref[rank] == 1
    partner = pairing_ref[rank]
    picks = []
    for order in (order_a, order_b):
        pick = 0
        for k, bit in enumerate(order):
            differs = lax.rem(rank // bit + partner // bit, 2)
            pick = pick + differs * (1 << k)
        picks.append(jnp.where(keep, 0, pick))
    levels = len(order_a)
    for tick in range(1, levels + len(groups)):
        for k, group in enumerate(groups):
            if 0 <= tick - k <= levels:
                advance(*near[group])
            if tick - k == levels:
                for at in range(PIECES)[group]:
                    kernels[at][place] = slots[at][picks[at % 2]]
                advance(*share_lines[group])
        if tick < levels + 1:
            advance(noise_line)
    loads[3].wait()
    half = moment_a.shape[1]
    moment_a[0] = cut(moment_ref, 0, half)
    moment_b[0] = cut(moment_ref, half, half)
    advance(third, fourth)

    def put(buffer, plane, value):
        columns = pl.ds((plane + 1) * X, X)
        low = jnp.where(lane == 0, 0.0, pltpu.roll(value, 1, 1))
        high = jnp.where(lane == X - 1, 0.0, pltpu.roll(value, X - 1, 1))
        buffer[0:wide, columns] = low.astype(jnp.bfloat16)
        buffer[wide : 2 * wide, columns] = value.astype(jnp.bfloat16)
        buffer[2 * wide : 3 * wide, columns] = high.astype(jnp.bfloat16)

    def near_rows(*rows):
        return jnp.concatenate(rows, axis=0).astype(jnp.float32)[:share_rows]

    def unpack(part):
        rows = near_rows(*[piece[part] for piece in kernels])
        begin = pl.multiple_of(2 * part * share_rows, 8)
        square_ref[pl.ds(begin, share_rows, stride=2), :] = rows[:, :channels]
        square_ref[pl.ds(begin + 1, share_rows, stride=2), :] = rows[:, channels:]

    def tap(layer, a, b, c):
        begin = (27 * layer + 9 * a + 3 * b + c) * channels
        return square_ref[begin : begin + channels, :]

    def prepare(layer):
        for a in range(3):
            for c in range(3):
                middle = tap(layer, a, 1, c)
                block = jnp.concatenate(
                    [
                        jnp.concatenate([middle, tap(layer, a, 2, c)], axis=1),
                        jnp.concatenate([tap(layer, a, 0, c), middle], axis=1),
                    ],
                    axis=0,
                )
                fore_ref[layer, a, :, c * wide : (c + 1) * wide] = block.astype(jnp.bfloat16)
                if layer:
                    back_ref[layer - 1, 2 - a, :, (2 - c) * wide : (3 - c) * wide] = (
                        block.T.astype(jnp.bfloat16)
                    )

    def convolved(weights, buffer, pair):
        total = None
        for a in range(3):
            columns = pl.ds((2 * pair + a) * X, 2 * X)
            term = dot(weights[a], buffer[:, columns])
            total = term if total is None else total + term
        return total

    def forward(layer):
        for pair in range(planes // 2):
            total = convolved(fore_ref.at[layer], inputs_ref.at[layer], pair)
            if layer < 2:
                pre_ref[layer, :, 2 * pair * X : (2 * pair + 2) * X] = total
                act = gelu_of(total)
                put(inputs_ref.at[layer + 1], 2 * pair, act[:, :X])
                put(inputs_ref.at[layer + 1], 2 * pair + 1, act[:, X:])
            else:
                criticise(pair, jnp.tanh(total))

    score = jnp.broadcast_to(score_ref[...], (X, X)).T

    def criticise(pair, made):
        rounded = made.astype(jnp.bfloat16)
        exact = rounded.astype(jnp.float32)
        for a in range(2):
            plane = rounded[:, a * X : (a + 1) * X]
            made_all[2 * pair + a, :, 0:X] = plane[:channels]
            made_all[2 * pair + a, :, X : 2 * X] = plane[channels:]
        pieces = []
        for a in range(2):
            plane = exact[:, a * X : (a + 1) * X]
            pieces += [plane, pltpu.roll(plane, X - 1, 1)]
        response = dot(critic_ref[...], jnp.concatenate(pieces, axis=0).astype(jnp.bfloat16))
        scores = jnp.sum(score * gelu_of(response), axis=0, keepdims=True)
        slope = -jax.nn.sigmoid(-scores)
        upstream = gelu_slope(response) * (slope * score)
        upstream = jnp.where(lax.rem(lane, 2) == 0, upstream, 0.0)
        pieces = jnp.concatenate([upstream, pltpu.roll(upstream, 1, 1)], axis=0)
        spread = dot(critic_back_ref[...], pieces.astype(jnp.bfloat16))
        for a in range(2):
            plane = made[:, a * X : (a + 1) * X]
            fall = 1.0 - plane * plane
            put(grads_ref.at[0], 2 * pair + a, spread[a * wide : (a + 1) * wide] * fall)

    unpack(place)
    while advance(noise_line):
        pass
    for part in range(depth):

        for plane in range(own):
            both = volume_ref[part, plane].astype(jnp.float32)
            whole = jnp.concatenate([both[:, :X], both[:, X:]], axis=0)
            put(inputs_ref.at[0], part * own + plane, whole)

    layer_rows = 27 * channels
    edges = []
    for layer in range(3):
        edges.append((layer * layer_rows // (2 * share_rows), ((layer + 1) * layer_rows - 1) // (2 * share_rows)))

    def known(layer, at):
        return max(abs(edge - at) for edge in edges[layer])

    def ready(layer, at):
        before = ready(layer - 1, at) if layer else 0
        last = known(layer, at)
        return max(before, layer + 1 if last <= layer + 1 < depth else depth - 1)

    for step in range(depth):
        if step:
            advance(*share_lines)
            advance(third, fourth)

            @pl.when(place >= step)
            def _():
                unpack(place - step)

            @pl.when(place + step <= depth - 1)
            def _():
                unpack(place + step)

        for act, due in ((prepare, known), (forward, ready)):
            for layer in range(3):
                places = [at for at in range(depth) if due(layer, at) == step]
                if places:
                    here = place == places[0]
                    for at in places[1:]:
                        here = here | (place == at)

                    @pl.when(here)
                    def _():
                        act(layer)

    begin = 2 * place * share_rows

    def kernel_sums(layer, gradient):
        for a in range(3):
            low = (27 * layer + 9 * a) * channels

            @pl.when((low + 9 * channels > begin) & (low < begin + 2 * share_rows))
            def _():
                sums = dot_rows(gradient[...], inputs_ref[layer, :, a * X : a * X + cells])
                for c in range(3):
                    block = sums[:, c * wide : (c + 1) * wide]
                    parts = (
                        block[channels:, :channels],
                        block[:channels, :channels] + block[channels:, channels:],
                        block[:channels, channels:],
                    )
                    for b in range(3):
                        row = low + (3 * b + c) * channels
                        square_ref[row : row + channels, :] = parts[b]

    for layer in (2, 1):
        held = grads_ref.at[2 - layer]
        kernel_sums(layer, held.at[wide : 2 * wide, X : X + cells])

        @pl.when(begin < layer * layer_rows)
        def _():
            for pair in range(planes // 2):
                columns = pl.ds(2 * pair * X, 2 * X)
                total = convolved(back_ref.at[layer - 1], held, pair)
                total = total * gelu_slope(pre_ref[layer - 1, :, columns])
                if layer == 2:
                    put(grads_ref.at[1], 2 * pair, total[:, :X])
                    put(grads_ref.at[1], 2 * pair + 1, total[:, X:])
                else:
                    later = pl.ds((2 * pair + 1) * X, 2 * X)
                    grads_ref[0, wide : 2 * wide, later] = total.astype(jnp.bfloat16)

    kernel_sums(0, grads_ref.at[0, wide : 2 * wide, X : X + cells])

    while advance(*share_lines, third, fourth):
        pass
    made_ref[...] = made_all[pl.ds(place * own, own)]
    sums = jnp.concatenate(
        [
            square_ref[pl.ds(begin, share_rows, stride=2), :],
            square_ref[pl.ds(begin + 1, share_rows, stride=2), :],
        ],
        axis=1,
    )

    def adopted(mine, near):
        return jnp.where(keep, mine, near)

    near_moment = near_rows(moment_a[picks[0]], moment_b[picks[1]])
    near_weight = near_rows(*[piece[place] for piece in kernels])
    moment = momentum_decay * adopted(moment_ref[...], near_moment) + sums
    new_moment_ref[...] = moment
    new_weight_ref[...] = adopted(weight_ref[...], near_weight) - step_length * moment


def on_device(trainers, depth, noise, gen_weight, gen_momentum, disc_weight, score_weight, pairing, flags):
    own, channels = noise.shape[1], noise.shape[2]
    planes = own * depth
    if planes > WHOLE_PLANES or depth < 2 or trainers & (trainers - 1):
        return on_device_split(
            noise, gen_weight, gen_momentum, disc_weight, score_weight, pairing, flags
        )
    weight, moment = gen_weight.reshape(-1, X), gen_momentum.reshape(-1, X)
    rows = weight.shape[0]
    half = -(-rows // 32) * 16
    units = -(-rows // 16)
    sizes = [16 * ((units + PIECES - 1 - k) // PIECES) for k in range(PIECES)]
    levels = trainers.bit_length() - 1
    wide = 2 * channels
    framed = (planes + 2) * X
    vmem = pl.BlockSpec(memory_space=pltpu.VMEM)
    smem = pl.BlockSpec(memory_space=pltpu.SMEM)
    hbm = pl.BlockSpec(memory_space=pltpu.HBM)
    moments = pltpu.VMEM((trainers, half, X), jnp.bfloat16)
    made, new_weight, new_moment = pl.pallas_call(
        functools.partial(round_kernel, trainers, depth),
        out_shape=(
            pltpu.VMEM(noise.shape[1:], jnp.bfloat16),
            pltpu.VMEM(weight.shape, jnp.float32),
            pltpu.VMEM(weight.shape, jnp.float32),
        ),
        in_specs=[smem] * 2 + [hbm] * 4 + [vmem],
        out_specs=(vmem,) * 3,
        scratch_shapes=[
            pltpu.VMEM(weight.shape, jnp.float32),
            pltpu.VMEM(weight.shape, jnp.float32),
            pltpu.VMEM((8, channels, X), jnp.bfloat16),
            pltpu.VMEM((depth,) + noise.shape[1:], jnp.bfloat16),
            moments,
            moments,
            pltpu.VMEM((81 * channels, channels), jnp.float32),
            pltpu.VMEM((3, 3, wide, 3 * wide), jnp.bfloat16),
            pltpu.VMEM((2, 3, wide, 3 * wide), jnp.bfloat16),
            pltpu.VMEM((3, 3 * wide, framed), jnp.bfloat16),
            pltpu.VMEM((2, 3 * wide, framed), jnp.bfloat16),
            pltpu.VMEM((2, wide, planes * X), jnp.float32),
            pltpu.VMEM((planes,) + noise.shape[2:], jnp.bfloat16),
            pltpu.VMEM((X, 4 * wide), jnp.bfloat16),
            pltpu.VMEM((2 * wide, 2 * X), jnp.bfloat16),
            pltpu.SemaphoreType.DMA((4,)),
            pltpu.SemaphoreType.DMA((PIECES + 2, levels)),
            pltpu.SemaphoreType.DMA((PIECES + 2, levels)),
            pltpu.SemaphoreType.DMA((4 * PIECES + 4, depth - 1)),
        ]
        + [pltpu.VMEM((trainers, size, X), jnp.bfloat16) for size in sizes]
        + [pltpu.VMEM((depth, size, X), jnp.bfloat16) for size in sizes],
        compiler_params=pltpu.CompilerParams(
            collective_id=0, has_side_effects=True, vmem_limit_bytes=VMEM_LIMIT
        ),
    )(
        pairing,
        flags,
        weight,
        moment,
        noise[0],
        disc_weight[0].swapaxes(1, 2),
        score_weight,
    )
    return made[None], new_weight.reshape(gen_weight.shape), new_moment.reshape(gen_weight.shape)


def solution(mesh):
    placed = (
        P("trainer", "depth", None, None),
        P("trainer", "depth"),
        P("trainer", "depth"),
        P("trainer", None, None, None),
        P("trainer", None),
        P(),
        P(),
    )
    return jax.shard_map(
        functools.partial(on_device, mesh.shape["trainer"], mesh.shape["depth"]),
        mesh=mesh,
        in_specs=placed,
        out_specs=(P("trainer", "depth", None, None), P("trainer", "depth"), P("trainer", "depth")),
        check_vma=False,
    )
```
